128 devices in a mesh: section: 16 (over z, y), tp: 8 (over x, core).
Axes of the slice: x: 4, y: 4, z: 4, core: 2. Of those that a mesh axis runs over, the one named last changes fastest.
Arguments:
- patch_states: bfloat16 [8192, 5120], P(('section', 'tp')), may hold values from -6 to 6
- merge_in: bfloat16 [5120, 5120], P(None, 'tp'), may hold values from -0.078125 to 0.078125
- merge_out: bfloat16 [5120, 8192], P('tp'), may hold values from -0.125 to 0.125
- kv_weight: bfloat16 [8192, 2048], P('tp'), may hold values from -0.09375 to 0.09375
- queries: bfloat16 [16, 16, 8192], P('section', None, 'tp'), may hold values from -90 to 90
- new_kv: bfloat16 [16, 16, 2048], P('section', None, 'tp'), may hold values from -8 to 8
- citations: int32 [128, 4], replicated, may hold values from 0 to 31, as said below
- lengths: int32 [128], replicated, may hold values from 3 to 4
- prefill_owner: int32 [128], replicated, may hold values from 0 to 15
- decode_owner: int32 [128], replicated, may hold values from 0 to 15, as said below
Outputs:
- attended: bfloat16 [16, 16, 8192], P('section', None, 'tp')
The draws below stay inside these ranges and needn't reach their ends.
Inputs may be any that keep to these rules, and one draw needn't show every extreme that they name: `citations`: row w lists frames of one camera, newest first; frame f is encoded by section index f // 2; the first lengths[w] entries are read. Over the windows of one prefill owner, the frames read hold at most one frame of each section index and at most 8 frames in all; both bounds are met in every draw. `decode_owner`: no two windows with the same prefill owner have the same decode owner.
All inputs are finite; a program needn't handle non-finite values.
Results may differ from the reference program's by a relative error of at most 0.035.
Values may be sent and summed in bfloat16 or wider, within the bound.
A program may use at most 128 MiB of HBM per device.

```python
import math
import jax
import jax.numpy as jnp
from jax import lax

VIT = 1280
MERGED = 5120
MH = 5120
D = 8192
QH = 64
KVH = 8
HD = 128
GRID = 16
FD = 2
CAMERAS = 8
FRAMES = 32
CITE = 4
WINDOWS = 128
N_SECTION = 16


def windows_plan(key):
    slot_total = N_SECTION * N_SECTION
    keys_list = jax.random.split(key, 7)
    forced = jax.random.randint(keys_list[0], (), 0, N_SECTION)
    ranking = jax.random.permutation(keys_list[1], slot_total) + 2
    slot_ids = jnp.arange(slot_total)
    ranking = jnp.where(slot_ids == forced * N_SECTION, 0, ranking)
    ranking = jnp.where(slot_ids == forced * N_SECTION + 1, 1, ranking)
    chosen = jnp.argsort(ranking)[:WINDOWS]
    chosen = chosen[jax.random.permutation(keys_list[2], WINDOWS)]
    owners = chosen // N_SECTION
    ranks = chosen % N_SECTION
    special = (owners == forced) & (ranks <= 1)
    decoders = (owners + ranks) % N_SECTION
    first_cam = jax.random.randint(keys_list[3], (N_SECTION,), 0, CAMERAS)
    second_cam = (first_cam + FD * jax.random.randint(keys_list[4], (N_SECTION,), 1, CAMERAS // FD)) % CAMERAS
    take_second = jax.random.randint(keys_list[5], (WINDOWS,), 0, 2)
    take_second = jnp.where(special, ranks, take_second)
    camera = jnp.where(take_second == 1, second_cam[owners], first_cam[owners])
    frame_count = jax.random.randint(keys_list[6], (WINDOWS,), max(1, CITE - 1), CITE + 1)
    frame_count = jnp.where(special, CITE, frame_count)
    list_pos = jnp.arange(CITE)
    cited = camera[:, None] + CAMERAS * (CITE - 1 - list_pos)[None, :]
    return (cited.astype(jnp.int32), frame_count.astype(jnp.int32), owners.astype(jnp.int32), decoders.astype(jnp.int32))


def draw_citations(key, part):
    plan = windows_plan(key)
    return plan[0]


def draw_lengths(key, part):
    plan = windows_plan(key)
    return plan[1]


def draw_prefill_owner(key, part):
    plan = windows_plan(key)
    return plan[2]


def draw_decode_owner(key, part):
    plan = windows_plan(key)
    return plan[3]


def draw_queries(key, part):
    key = jax.random.fold_in(key, 11)
    base_key = jax.random.fold_in(key, 0)
    shape = (N_SECTION, N_SECTION, QH * HD)
    values = jax.random.normal(base_key, shape, jnp.float32) * 4.0
    return jnp.clip(values, -90.0, 90.0).astype(jnp.bfloat16)


def raised(values, rng, source, target, blocks, factor):
    def block_of(dim):
        return (jnp.arange(values.shape[dim]) // (values.shape[dim] // blocks)).reshape((-1,) + (1,) * (values.ndim - 1 - dim))

    first = jax.random.permutation(rng, blocks)[block_of(target)]
    other_side = (block_of(target) + blocks // 2) % blocks
    return jnp.where((block_of(source) == first) | (block_of(source) == other_side), factor * values, values)


def shard_levels(rng, extent, pieces, least, top_value):
    factor_of, own = 1.0, jax.random.fold_in(rng, 6)
    for dim, blocks in pieces:
        steps = jnp.exp(jax.random.uniform(jax.random.fold_in(own, dim), (blocks,), jnp.float32, least / len(pieces), top_value / len(pieces)))
        factor_of = factor_of * jnp.repeat(steps, extent[dim] // blocks).reshape([-1 if axis == dim else 1 for axis in range(len(extent))])
    return factor_of


def normal_values(rng, shape, scale, reach, shards=(), dtype=jnp.bfloat16):
    values = jax.random.normal(rng, shape, jnp.float32) * scale
    if len(shards) > 0:
        values = shard_levels(rng, shape, shards, -0.22, 0.18) * values
    return jnp.clip(values, min=-reach, max=reach).astype(dtype)


def heavy_noise(key, extent, deviation, most, cuts, heavy, kind=jnp.bfloat16):
    drawn = deviation * jax.random.normal(key, extent, jnp.float32)
    if cuts:
        drawn = drawn * shard_levels(key, extent, cuts, -0.22, 0.18)
    return jnp.clip(raised(drawn, jax.random.fold_in(key, 3), *heavy), -most, most).astype(kind)


def setup_inputs(seed: int = 0) -> dict:
    seeds = jax.random.split(jax.random.key(seed), 11)
    return {
        "patch_states": normal_values(seeds[0], (FRAMES * GRID * GRID, MERGED), 1.0, 6.0, ((0, 128),)),
        "merge_in": normal_values(seeds[1], (MERGED, MH), MERGED ** -0.5, 0.078125, ((1, 8),)),
        "merge_out": heavy_noise(seeds[2], (MH, D), MH ** -0.5, 0.125, ((0, 8),), (0, 1, 8, 2.0)),
        "kv_weight": heavy_noise(seeds[3], (D, KVH * 2 * HD), D ** -0.5, 0.09375, ((0, 8),), (0, 1, 8, 2.0)),
        "queries": draw_queries(jax.random.fold_in(seeds[10], 71), 0),
        "new_kv": normal_values(seeds[5], (N_SECTION, N_SECTION, KVH * 2 * HD), 1.5, 8.0, ((0, 16), (2, 8))),
        "citations": draw_citations(jax.random.fold_in(seeds[10], 71), 0),
        "lengths": draw_lengths(jax.random.fold_in(seeds[10], 71), 0),
        "prefill_owner": draw_prefill_owner(jax.random.fold_in(seeds[10], 71), 0),
        "decode_owner": draw_decode_owner(jax.random.fold_in(seeds[10], 71), 0),
    }


def rotation_angles(offsets):
    half_width = HD // 2
    freq_slot = jnp.arange(half_width)
    inverse = jnp.exp(freq_slot.astype(jnp.float32) * (-2.0 * math.log(1000000.0) / HD))
    position = jnp.arange(GRID * GRID)
    height = (position // GRID).astype(jnp.float32)
    across = (position % GRID).astype(jnp.float32)
    first_cut = HD // 8
    second_cut = first_cut + 3 * HD // 16
    spatial = jnp.where(freq_slot[None, :] < second_cut, height[:, None], across[:, None])
    temporal = offsets.astype(jnp.float32)[..., None, None]
    placed = jnp.where(freq_slot < first_cut, temporal, spatial)
    return placed * inverse

def rotate_keys(key_rows, angles):
    half_width = key_rows.shape[-1] // 2
    cosine = jnp.cos(angles)
    sine_part = jnp.sin(angles)
    first_half = key_rows[..., :half_width]
    second_half = key_rows[..., half_width:]
    return jnp.concatenate([first_half * cosine - second_half * sine_part, second_half * cosine + first_half * sine_part], axis=-1)

def reference(patch_states, merge_in, merge_out, kv_weight, queries, new_kv, citations, lengths, prefill_owner, decode_owner):
    row_count = patch_states.shape[0]
    blocks = patch_states.astype(jnp.float32).reshape(row_count, -1, VIT)
    centered = blocks - lax.optimization_barrier(jnp.mean(blocks, axis=-1, keepdims=True))
    variance = lax.optimization_barrier(jnp.mean(centered * centered, axis=-1, keepdims=True))
    normed = (centered * lax.rsqrt(variance + 1e-06)).reshape(row_count, MERGED).astype(jnp.bfloat16)
    hidden = jax.nn.gelu(jnp.dot(normed, merge_in, preferred_element_type=jnp.float32), approximate=False).astype(jnp.bfloat16)
    merged = jnp.dot(hidden, merge_out, preferred_element_type=jnp.float32).astype(jnp.bfloat16)
    frame_kv = jnp.dot(merged, kv_weight, preferred_element_type=jnp.float32).astype(jnp.bfloat16).reshape(FRAMES, GRID * GRID, KVH, 2, HD)
    heads_per = QH // KVH
    inv_root = 1.0 / math.sqrt(HD)

    def one_window(window_id):
        cited = citations[window_id]
        frame_count = lengths[window_id]
        fetched = frame_kv[cited]
        list_pos = jnp.arange(CITE)
        angles = rotation_angles(frame_count - 1 - list_pos)
        page_keys = rotate_keys(fetched[:, :, :, 0, :].astype(jnp.float32), angles[:, :, None, :]).astype(jnp.bfloat16)
        page_values = fetched[:, :, :, 1, :]
        target = decode_owner[window_id]
        source = prefill_owner[window_id]
        query_rows = queries[target, source].astype(jnp.float32).reshape(KVH, heads_per, HD)
        own_pair = new_kv[target, source].astype(jnp.float32).reshape(KVH, 2, HD)
        scores = jnp.einsum('hgd,jthd->hgjt', query_rows, page_keys.astype(jnp.float32)) * inv_root
        usable = (list_pos < frame_count)[None, None, :, None]
        scores = jnp.where(usable, scores, -jnp.inf)
        own_score = jnp.einsum('hgd,hd->hg', query_rows, own_pair[:, 0, :]) * inv_root
        highest = jnp.maximum(lax.optimization_barrier(jnp.max(scores, axis=(2, 3))), own_score)
        weights = jnp.exp(scores - highest[:, :, None, None])
        own_weight = jnp.exp(own_score - highest)
        denominator = lax.optimization_barrier(jnp.sum(weights, axis=(2, 3))) + own_weight
        weights = (weights / denominator[:, :, None, None]).astype(jnp.bfloat16)
        own_weight = (own_weight / denominator).astype(jnp.bfloat16)
        result = jnp.einsum('hgjt,jthd->hgd', weights.astype(jnp.float32), page_values.astype(jnp.float32))
        result = result + own_weight.astype(jnp.float32)[:, :, None] * own_pair[:, 1, :][:, None, :]
        return result.reshape(QH * HD).astype(jnp.bfloat16)
    results = lax.map(one_window, jnp.arange(WINDOWS))
    attended = jnp.zeros((N_SECTION, N_SECTION, QH * HD), jnp.bfloat16)
    return attended.at[decode_owner, prefill_owner].set(results)
```

```python
import math

import jax
import jax.numpy as jnp
import numpy as np
from jax import lax
from jax.experimental import pallas as pl
from jax.experimental.pallas import tpu as pltpu
from jax.sharding import PartitionSpec as P

F32 = jnp.float32
BF16 = jnp.bfloat16
VIT = 1280
HD = 128
GRID = 16
NS = 16
CITE = 4
ROWS = 64
GROUP = 128
TOKENS = 512
KIN = 5120
HU = 640
KVB = 1024
HALF = HU // 2
QUARTER = HU // 4
PART = 144


def tables():
    slot = np.arange(HD // 2)
    inverse = np.exp(slot.astype(np.float32) * np.float32(-2.0 * math.log(1000000.0) / HD)).astype(np.float32)
    token = np.arange(GRID * GRID)
    height = (token // GRID).astype(np.float32)
    across = (token % GRID).astype(np.float32)
    first = HD // 8
    second = first + 3 * HD // 16
    spatial = np.where(slot[None, :] < second, height[:, None], across[:, None])
    spatial = np.where(slot[None, :] < first, np.float32(0.0), spatial) * inverse[None, :]
    cosine, sine = np.cos(spatial), np.sin(spatial)
    keys = np.stack([np.concatenate([cosine, cosine], 1), np.concatenate([-sine, sine], 1)])
    steps = np.arange(CITE).astype(np.float32)[:, None] * inverse[None, :]
    steps = np.where(slot[None, :] < first, steps, np.float32(0.0))
    cosine, sine = np.cos(steps), np.sin(steps)
    asks = np.stack([np.concatenate([cosine, cosine], 1), np.concatenate([sine, -sine], 1)])
    return keys.astype(np.float32), asks.astype(np.float32)


class Counter:
    def __init__(self):
        self.n = 0

    def take(self, k=1):
        first = self.n
        self.n += k
        return first


N_SEND = 160
N_RECV = 160
N_LOCAL = 8


def kernel(
    patch, w1, w2, kvw, q, nkv, meta, ktab, qtab, out,
    rows, w1v, w2v, kvg, wacc, wg, hacc, mine, psend, precv, h1s, h1r, h2s, h2r,
    kbuf, vbuf, vt, qg, osend, orecv, ssem, rsem, lsem,
):
    s = lax.axis_index("section")
    t = lax.axis_index("tp")
    x, c = t // 2, t % 2
    z, y = s // 4, s % 4
    mate = 2 * x + (1 - c)
    cr, cl, co = (x + 1) % 4, (x + 3) % 4, (x + 2) % 4
    xr, xl, xo = 2 * cr + c, 2 * cl + c, 2 * co + c
    yn, yp, yo = (y + 1) % 4, (y + 3) % 4, (y + 2) % 4
    zn, zp, zo = (z + 1) % 4, (z + 3) % 4, (z + 2) % 4
    sends, recvs = Counter(), Counter()
    pending = []

    def to_tp(who):
        return {"tp": who}

    def to_section(who):
        return {"section": who}

    def start(src, dst, slot, dev):
        copy = pltpu.make_async_remote_copy(
            src_ref=src, dst_ref=dst, send_sem=ssem.at[sends.take()], recv_sem=rsem.at[slot],
            device_id=dev, device_id_type=pl.DeviceIdType.MESH,
        )
        copy.start()
        pending.append(copy)

    def arrive(dst, slot):
        pltpu.make_async_remote_copy(
            src_ref=dst, dst_ref=dst, send_sem=ssem.at[0], recv_sem=rsem.at[slot],
            device_id=to_tp(mate), device_id_type=pl.DeviceIdType.MESH,
        ).wait_recv()

    load1 = pltpu.make_async_copy(w1, w1v, lsem.at[0])
    load2 = pltpu.make_async_copy(w2, w2v, lsem.at[1])
    cols = pl.ds(pl.multiple_of(s * HD, HD), HD)

    def kv_at(b, h=None):
        if h is None:
            return kvg.at[pl.ds(pl.multiple_of(b * KVB, KVB), KVB), :]
        return kvg.at[pl.ds(pl.multiple_of(b * KVB + h * (KVB // 2), KVB // 2), KVB // 2), :]

    def kv_own(h=None):
        if h is None:
            return kvw.at[:, cols]
        return kvw.at[pl.ds(h * (KVB // 2), KVB // 2), cols]

    def rows_at(b, h=None):
        if h is None:
            return rows.at[pl.ds(pl.multiple_of(b * ROWS, ROWS), ROWS), :]
        return rows.at[pl.ds(pl.multiple_of(b * ROWS + h * (ROWS // 2), ROWS // 2), ROWS // 2), :]

    load3 = pltpu.make_async_copy(kv_own(), kv_at(t), lsem.at[2])
    load4 = pltpu.make_async_copy(q, qg.at[s], lsem.at[3])
    load3.start()
    load4.start()
    load2.start()
    load1.start()

    barrier = pltpu.get_barrier_semaphore()
    for who in (mate, xr, xl):
        pl.semaphore_signal(barrier, inc=1, device_id=to_tp(who), device_id_type=pl.DeviceIdType.MESH)

    @pl.loop(1, NS)
    def _(i):
        pl.semaphore_signal(
            barrier, inc=1, device_id=to_section((s + i) % NS), device_id_type=pl.DeviceIdType.MESH
        )

    pl.semaphore_wait(barrier, 3 + NS - 1)

    class Ring:
        def __init__(self, at):
            self.at = at
            self.base = recvs.take(10)

        def open(self, own):
            b = self.base
            start(own(0), self.at(t, 0), b + 0, to_tp(xr))
            start(own(1), self.at(t, 1), b + 3, to_tp(xl))
            start(own(1), self.at(t, 1), b + 1, to_tp(xr))
            start(own(0), self.at(t, 0), b + 2, to_tp(xl))
            start(own(None), self.at(t), b + 6, to_tp(mate))

        def forward(self):
            b = self.base
            arrive(self.at(xl, 0), b + 0)
            start(self.at(xl, 0), self.at(xl, 0), b + 4, to_tp(xr))
            arrive(self.at(xr, 1), b + 3)
            start(self.at(xr, 1), self.at(xr, 1), b + 5, to_tp(xl))

        def near(self):
            b = self.base
            arrive(self.at(xl, 1), b + 1)
            start(self.at(xl), self.at(xl), b + 7, to_tp(mate))
            arrive(self.at(xr, 0), b + 2)
            start(self.at(xr), self.at(xr), b + 8, to_tp(mate))

        def far(self):
            b = self.base
            arrive(self.at(xo, 0), b + 4)
            arrive(self.at(xo, 1), b + 5)
            start(self.at(xo), self.at(xo), b + 9, to_tp(mate))

        def mates(self, k):
            chip = (x, cl, cr, co)[k]
            arrive(self.at(2 * chip + (1 - c)), self.base + 6 + k)

    kv_ring = Ring(kv_at)
    kv_ring.open(kv_own)

    q_base = recvs.take(NS)
    q_send = sends.take(NS)

    def q_copy(i):
        return pltpu.make_async_remote_copy(
            src_ref=q, dst_ref=qg.at[s], send_sem=ssem.at[q_send + i], recv_sem=rsem.at[q_base + i],
            device_id=to_section((s + i) % NS), device_id_type=pl.DeviceIdType.MESH,
        )

    @pl.loop(1, NS)
    def _(i):
        q_copy(i).start()

    for b in range(KIN // VIT):
        span = pl.ds(b * VIT, VIT)
        block = patch[:, span].astype(F32)
        centered = block - jnp.mean(block, axis=-1, keepdims=True)
        variance = jnp.mean(centered * centered, axis=-1, keepdims=True)
        rows[pl.ds(pl.multiple_of(t * ROWS, ROWS), ROWS), span] = (
            centered * lax.rsqrt(variance + 1e-06)
        ).astype(BF16)

    kv_ring.forward()
    row_ring = Ring(rows_at)
    row_ring.open(lambda h: rows_at(t, h))

    def w_step(b, first=False):
        part = jnp.dot(
            w2v[:, pl.ds(pl.multiple_of(b * KVB, KVB), KVB)],
            kvg[pl.ds(pl.multiple_of(b * KVB, KVB), KVB), :],
            preferred_element_type=F32,
        )
        if first:
            wacc[...] = part
        else:
            wacc[...] += part

    load3.wait()
    load2.wait()
    w_step(t, first=True)
    kv_ring.mates(0)
    w_step(mate)
    kv_ring.near()
    w_step(xl)
    w_step(xr)
    kv_ring.far()
    w_step(xo)
    kv_ring.mates(1)
    w_step(2 * cl + (1 - c))
    kv_ring.mates(2)
    w_step(2 * cr + (1 - c))
    kv_ring.mates(3)
    w_step(2 * co + (1 - c))

    def lanes(yy):
        return pl.ds(pl.multiple_of((yy % 2) * HD, HD), HD)

    def block_at(zz, yy, r0, n):
        return wg.at[zz, yy // 2, pl.ds(r0, n), lanes(yy)]

    def line_at(zz, r0, n):
        return wg.at[zz, :, pl.ds(r0, n), :]

    def column_at(yy, r0, n):
        return wg.at[:, yy // 2, pl.ds(r0, n), lanes(yy)]

    def sec(zz, yy):
        return to_section(zz * 4 + yy)

    wg[z, y // 2, :, lanes(y)] = wacc[...].astype(BF16)

    class Cross:
        def __init__(self, at, me, nxt, prv, opp, dev_n, dev_p, r0):
            self.at, self.me, self.nxt, self.prv, self.opp = at, me, nxt, prv, opp
            self.dev_n, self.dev_p, self.r0 = dev_n, dev_p, r0
            self.base = recvs.take(4)

        def open(self):
            b, own = self.base, self.at(self.me, self.r0, HALF)
            start(own, own, b + 0, self.dev_n)
            start(own, own, b + 1, self.dev_p)

        def forward(self):
            b = self.base
            arrive(self.at(self.prv, self.r0, HALF), b + 0)
            low = self.at(self.prv, self.r0, QUARTER)
            start(low, low, b + 2, self.dev_n)
            arrive(self.at(self.nxt, self.r0, HALF), b + 1)
            high = self.at(self.nxt, self.r0 + QUARTER, QUARTER)
            start(high, high, b + 3, self.dev_p)

        def finish(self):
            b = self.base
            arrive(self.at(self.opp, self.r0, QUARTER), b + 2)
            arrive(self.at(self.opp, self.r0 + QUARTER, QUARTER), b + 3)

    y_first = Cross(lambda yy, r, n: block_at(z, yy, r, n), y, yn, yp, yo, sec(z, yn), sec(z, yp), 0)
    z_first = Cross(lambda zz, r, n: block_at(zz, y, r, n), z, zn, zp, zo, sec(zn, y), sec(zp, y), HALF)
    z_then = Cross(line_at, z, zn, zp, zo, sec(zn, y), sec(zp, y), 0)
    y_then = Cross(column_at, y, yn, yp, yo, sec(z, yn), sec(z, yp), HALF)
    y_first.open()
    z_first.open()

    def hidden(g):
        r = pl.ds(pl.multiple_of(g * GROUP, GROUP), GROUP)

        def part(k):
            span = pl.ds(pl.multiple_of(k * 1024, 1024), 1024)
            return jnp.dot(rows[r, span], w1v[span, :], preferred_element_type=F32)

        hacc[g] = part(0)

        @pl.loop(1, KIN // 1024)
        def _(k):
            hacc[g] += part(k)

    p_base = recvs.take(4)
    p_send = sends.take(4)

    def pair_copy(k, g):
        return pltpu.make_async_remote_copy(
            src_ref=psend.at[g], dst_ref=precv.at[g], send_sem=ssem.at[p_send + k],
            recv_sem=rsem.at[p_base + k], device_id=to_tp(mate), device_id_type=pl.DeviceIdType.MESH,
        )

    def project(k, g):
        pre = hacc[g]
        hid = (0.5 * pre * (1.0 + lax.erf(pre * np.float32(math.sqrt(0.5))))).astype(BF16)
        for xx in range(4):
            psend[g, xx] = jnp.dot(hid, wg[xx, 1 - c], preferred_element_type=F32).astype(BF16)
        pair_copy(k, g).start()
        for xx in range(4):
            mine[g, xx] = jnp.dot(hid, wg[xx, c], preferred_element_type=F32)

    h1_base = recvs.take(8)
    h1_send = sends.take(8)
    h2_base = recvs.take(8)
    h2_send = sends.take(8)

    def hop(src, dst, ssl, rsl, way, g):
        return pltpu.make_async_remote_copy(
            src_ref=src.at[way, g], dst_ref=dst.at[way, g], send_sem=ssem.at[ssl + way * 4 + g],
            recv_sem=rsem.at[rsl + way * 4 + g], device_id=to_tp((xr, xl)[way]),
            device_id_type=pl.DeviceIdType.MESH,
        )

    def hop1(way, g):
        return hop(h1s, h1r, h1_send, h1_base, way, g)

    def hop2(way, g):
        return hop(h2s, h2r, h2_send, h2_base, way, g)

    def pair_sum(k, g):
        pair_copy(k, g).wait_recv()
        for xx in range(4):
            mine[g, xx] += precv[g, xx].astype(F32)
        for way in range(2):
            h1s[way, g] = mine[g, co, way * ROWS : (way + 1) * ROWS, :].astype(BF16)
            hop1(way, g).start()

    def middle(g):
        for way in range(2):
            hop1(way, g).wait_recv()
            dest = (cr, cl)[way]
            near, other = way * ROWS, (1 - way) * ROWS
            h2s[way, g, near : near + ROWS, :] = (
                mine[g, dest, near : near + ROWS, :] + h1r[way, g].astype(F32)
            ).astype(BF16)
            h2s[way, g, other : other + ROWS, :] = mine[g, dest, other : other + ROWS, :].astype(BF16)
            hop2(way, g).start()

    def last(g):
        hop2(0, g).wait_recv()
        hop2(1, g).wait_recv()
        total = mine[g, x] + h2r[0, g].astype(F32) + h2r[1, g].astype(F32)
        key = total[:, :HD]
        r = pl.ds(pl.multiple_of(g * GROUP, GROUP), GROUP)
        place = pl.ds(pl.multiple_of((g % 2) * GROUP, GROUP), GROUP)
        kbuf[r, :] = (key * ktab[0, place, :] + pltpu.roll(key, HD // 2, 1) * ktab[1, place, :]).astype(BF16)
        vt[:, r] = total[:, HD:].T.astype(BF16)

    load1.wait()
    row_ring.mates(0)
    hidden(x)
    y_first.forward()
    z_first.forward()
    row_ring.forward()
    y_first.finish()
    z_first.finish()
    z_then.open()
    y_then.open()
    row_ring.near()
    z_then.forward()
    y_then.forward()
    row_ring.mates(1)
    hidden(cl)
    row_ring.mates(2)
    hidden(cr)
    z_then.finish()
    y_then.finish()
    project(0, x)
    project(1, cl)
    pair_sum(0, x)
    project(2, cr)
    pair_sum(1, cl)
    row_ring.far()
    pair_sum(2, cr)
    row_ring.mates(3)
    hidden(co)
    project(3, co)
    pair_sum(3, co)
    order = (x, cl, cr, co)
    for g in order:
        middle(g)
    for g in order:
        last(g)

    load4.wait()

    @pl.loop(1, NS)
    def _(i):
        q_copy(i).wait_recv()

    inv_root = np.float32(1.0 / math.sqrt(HD))
    cited = [meta[:, j : j + 1] for j in range(CITE)]
    counts, prefill, decode = meta[:, 4:5], meta[:, 5:6], meta[:, 6:7]
    code = jnp.zeros((HD, 1), F32)
    for j in range(CITE):
        hit = (counts > j) & ((cited[j] // 2) == s)
        code += jnp.where(hit, (1 + (cited[j] % 2) + 2 * (counts - 1 - j)).astype(F32), 0.0)
    lane = lax.broadcasted_iota(jnp.int32, (HD, HD), 1)
    sub = lax.broadcasted_iota(jnp.int32, (HD, HD), 0)
    eye = lane == sub
    mine_o = prefill == (lane % NS)

    def heads_down(block):
        return jnp.concatenate([block[:, h * HD : (h + 1) * HD] for h in range(8)], axis=0)

    o_base = recvs.take(NS)
    o_send = sends.take(NS)

    def part_of(d):
        row = jnp.sum(jnp.where(mine_o & (decode == d), code, 0.0), axis=0, keepdims=True)
        col = jnp.sum(jnp.where(eye, row, 0.0), axis=1, keepdims=True)
        cosine, sine = qtab[0, 0:1, :], qtab[1, 0:1, :]
        for p in range(1, CITE):
            now = (col == 1.0 + 2.0 * p) | (col == 2.0 + 2.0 * p)
            cosine = jnp.where(now, qtab[0, p : p + 1, :], cosine)
            sine = jnp.where(now, qtab[1, p : p + 1, :], sine)
        asks = heads_down(qg[d].astype(F32))
        asks = (asks * cosine + pltpu.roll(asks, HD // 2, 1) * sine).astype(BF16)
        scores = lax.dot_general(kbuf[...], asks, (((1,), (1,)), ((), ())), preferred_element_type=F32)
        second = (row == 2.0) | (row == 4.0) | (row == 6.0) | (row == 8.0)
        frame = jnp.where(second, scores[256:], scores[:256]) * inv_root
        top = jnp.max(frame, axis=0, keepdims=True)
        weight = jnp.exp(frame - top)
        total = jnp.sum(weight, axis=0, keepdims=True)
        both = jnp.concatenate([jnp.where(second, 0.0, weight), jnp.where(second, weight, 0.0)], axis=0)
        value = jnp.dot(vt[...], both.astype(BF16), preferred_element_type=F32) / total
        live = row > 0.0
        osend[d, 0:HD, :] = jnp.where(live, value, 0.0).astype(BF16)
        level = jnp.where(live, top + jnp.log(total), -1e30)
        high = level.astype(BF16).astype(F32)
        mid = (level - high).astype(BF16).astype(F32)
        low = level - high - mid
        pad = jnp.zeros((PART - HD - 3, HD), F32)
        osend[d, HD:PART, :] = jnp.concatenate([high, mid, low, pad], axis=0).astype(BF16)

    def part_copy(i):
        d = (s + i) % NS
        return pltpu.make_async_remote_copy(
            src_ref=osend.at[d], dst_ref=orecv.at[s], send_sem=ssem.at[o_send + i],
            recv_sem=rsem.at[o_base + i], device_id=to_section(d), device_id_type=pl.DeviceIdType.MESH,
        )

    @pl.loop(1, NS)
    def _(i):
        part_of((s + i) % NS)
        part_copy(i).start()

    part_of(s)
    keep = pltpu.make_async_copy(osend.at[s], orecv.at[s], lsem.at[4])
    keep.start()

    asks = heads_down(q[...].astype(F32)).astype(BF16)
    own = lax.dot_general(nkv[:, :HD], asks, (((1,), (1,)), ((), ())), preferred_element_type=F32)
    pick = (lax.broadcasted_iota(jnp.int32, (NS, HD), 1) % NS) == lax.broadcasted_iota(jnp.int32, (NS, HD), 0)
    own = jnp.sum(jnp.where(pick, own, 0.0), axis=0, keepdims=True) * inv_root
    value = nkv[:, HD:].astype(F32)
    value = jnp.concatenate([value] * 8, axis=0).T
    present = jnp.sum(jnp.where(mine_o & (decode == s), 1.0, 0.0), axis=0, keepdims=True)

    keep.wait()

    @pl.loop(1, NS)
    def _(i):
        part_copy(i).wait_recv()

    tail = [orecv[j, HD:PART, :].astype(F32) for j in range(NS)]
    level = [v[0:1] + v[1:2] + v[2:3] for v in tail]
    top = own
    for v in level:
        top = jnp.maximum(top, v)
    weight = jnp.exp(own - top)
    total, value = weight, value * weight
    for j in range(NS):
        weight = jnp.exp(level[j] - top)
        total += weight
        value += orecv[j, 0:HD, :].astype(F32) * weight
    value = jnp.where(present > 0.0, value / total, 0.0).T
    for h in range(8):
        out[:, h * HD : (h + 1) * HD] = value[h * NS : (h + 1) * NS, :].astype(BF16)

    for copy in pending:
        copy.wait_send()
    for k, g in enumerate(order):
        pair_copy(k, g).wait_send()
        for way in range(2):
            hop1(way, g).wait_send()
            hop2(way, g).wait_send()

    @pl.loop(1, NS)
    def _(i):
        q_copy(i).wait_send()
        part_copy(i).wait_send()

    assert sends.n <= N_SEND and recvs.n <= N_RECV


def shards(
    patch_states, merge_in, merge_out, kv_weight, queries, new_kv, citations, lengths, prefill_owner, decode_owner
):
    meta = jnp.concatenate(
        [citations, lengths[:, None], prefill_owner[:, None], decode_owner[:, None], decode_owner[:, None]], axis=1
    )
    keys, asks = tables()
    vmem = pl.BlockSpec(memory_space=pltpu.VMEM)
    anywhere = pl.BlockSpec(memory_space=pl.ANY)
    result = pl.pallas_call(
        kernel,
        out_shape=jax.ShapeDtypeStruct((NS, 8 * HD), BF16),
        in_specs=[vmem, anywhere, anywhere, anywhere, vmem, vmem, vmem, vmem, vmem],
        out_specs=vmem,
        scratch_shapes=[
            pltpu.VMEM((TOKENS, KIN), BF16),
            pltpu.VMEM((KIN, HU), BF16),
            pltpu.VMEM((HU, 8192), BF16),
            pltpu.VMEM((8192, HD), BF16),
            pltpu.VMEM((HU, HD), F32),
            pltpu.VMEM((4, 2, HU, 2 * HD), BF16),
            pltpu.VMEM((4, GROUP, HU), F32),
            pltpu.VMEM((4, 4, GROUP, 2 * HD), F32),
            pltpu.VMEM((4, 4, GROUP, 2 * HD), BF16),
            pltpu.VMEM((4, 4, GROUP, 2 * HD), BF16),
            pltpu.VMEM((2, 4, ROWS, 2 * HD), BF16),
            pltpu.VMEM((2, 4, ROWS, 2 * HD), BF16),
            pltpu.VMEM((2, 4, GROUP, 2 * HD), BF16),
            pltpu.VMEM((2, 4, GROUP, 2 * HD), BF16),
            pltpu.VMEM((TOKENS, HD), BF16),
            pltpu.VMEM((8, HD), BF16),
            pltpu.VMEM((HD, TOKENS), BF16),
            pltpu.VMEM((NS, NS, 8 * HD), BF16),
            pltpu.VMEM((NS, PART, HD), BF16),
            pltpu.VMEM((NS, PART, HD), BF16),
            pltpu.SemaphoreType.DMA((N_SEND,)),
            pltpu.SemaphoreType.DMA((N_RECV,)),
            pltpu.SemaphoreType.DMA((N_LOCAL,)),
        ],
        compiler_params=pltpu.CompilerParams(
            collective_id=0, has_side_effects=True, vmem_limit_bytes=58 * 1024 * 1024
        ),
    )(
        patch_states, merge_in, merge_out, kv_weight, queries[0], new_kv[0], meta,
        jnp.asarray(keys), jnp.asarray(asks),
    )
    return result[None]


def solution(mesh):
    return jax.shard_map(
        shards,
        mesh=mesh,
        in_specs=(
            P(("section", "tp"), None),
            P(None, "tp"),
            P("tp", None),
            P("tp", None),
            P("section", None, "tp"),
            P("section", None, "tp"),
            P(),
            P(),
            P(),
            P(),
        ),
        out_specs=P("section", None, "tp"),
        check_vma=False,
    )
```

```python
import math

import jax
import jax.numpy as jnp
import numpy as np
from jax import lax
from jax.experimental import pallas as pl
from jax.experimental.pallas import tpu as pltpu
from jax.sharding import PartitionSpec as P

F32 = jnp.float32
BF16 = jnp.bfloat16
VIT = 1280
HD = 128
GRID = 16
NS = 16
CITE = 4
ROWS = 64
GROUP = 128
TOKENS = 512
KIN = 5120
HU = 640
KVB = 1024
HALF = HU // 2
QUARTER = HU // 4
PART = 144


def tables():
    slot = np.arange(HD // 2)
    inverse = np.exp(slot.astype(np.float32) * np.float32(-2.0 * math.log(1000000.0) / HD)).astype(np.float32)
    token = np.arange(GRID * GRID)
    height = (token // GRID).astype(np.float32)
    across = (token % GRID).astype(np.float32)
    first = HD // 8
    second = first + 3 * HD // 16
    spatial = np.where(slot[None, :] < second, height[:, None], across[:, None])
    spatial = np.where(slot[None, :] < first, np.float32(0.0), spatial) * inverse[None, :]
    cosine, sine = np.cos(spatial), np.sin(spatial)
    keys = np.stack([np.concatenate([cosine, cosine], 1), np.concatenate([-sine, sine], 1)])
    steps = np.arange(CITE).astype(np.float32)[:, None] * inverse[None, :]
    steps = np.where(slot[None, :] < first, steps, np.float32(0.0))
    cosine, sine = np.cos(steps), np.sin(steps)
    asks = np.stack([np.concatenate([cosine, cosine], 1), np.concatenate([sine, -sine], 1)])
    return keys.astype(np.float32), asks.astype(np.float32)


class Counter:
    def __init__(self):
        self.n = 0

    def take(self, k=1):
        first = self.n
        self.n += k
        return first


N_SEND = 104
N_RECV = 104
N_LOCAL = 8


def kernel(
    patch, w1, w2, kvw, q, nkv, cites, lens, prefills, decodes, ktab, qtab, out,
    rows, w1v, w2v, kvg, wacc, wg, hacc, hidb, mine, psend, precv, h1s, h1r, h2s, h2r,
    kbuf, vt, qg, askb, codeb, osend, orecv, ssem, rsem, lsem,
):
    s = lax.axis_index("section")
    t = lax.axis_index("tp")
    x, c = t // 2, t % 2
    z, y = s // 4, s % 4
    mate = 2 * x + (1 - c)
    cr, cl, co = (x + 1) % 4, (x + 3) % 4, (x + 2) % 4
    xr, xl, xo = 2 * cr + c, 2 * cl + c, 2 * co + c
    yn, yp, yo = (y + 1) % 4, (y + 3) % 4, (y + 2) % 4
    zn, zp, zo = (z + 1) % 4, (z + 3) % 4, (z + 2) % 4
    sends, recvs = Counter(), Counter()
    pending = []

    def to_tp(who):
        return {"tp": who}

    def to_section(who):
        return {"section": who}

    def start(src, dst, slot, dev):
        copy = pltpu.make_async_remote_copy(
            src_ref=src, dst_ref=dst, send_sem=ssem.at[sends.take()], recv_sem=rsem.at[slot],
            device_id=dev, device_id_type=pl.DeviceIdType.MESH,
        )
        copy.start()
        pending.append(copy)

    def arrive(dst, slot):
        pltpu.make_async_remote_copy(
            src_ref=dst, dst_ref=dst, send_sem=ssem.at[0], recv_sem=rsem.at[slot],
            device_id=to_tp(mate), device_id_type=pl.DeviceIdType.MESH,
        ).wait_recv()

    load1 = pltpu.make_async_copy(w1, w1v, lsem.at[0])
    load2 = pltpu.make_async_copy(w2, w2v, lsem.at[1])
    cols = pl.ds(pl.multiple_of(s * HD, HD), HD)

    def kv_at(b, h=None):
        if h is None:
            return kvg.at[pl.ds(pl.multiple_of(b * KVB, KVB), KVB), :]
        return kvg.at[pl.ds(pl.multiple_of(b * KVB + h * (KVB // 2), KVB // 2), KVB // 2), :]

    def rows_at(b, h=None):
        if h is None:
            return rows.at[pl.ds(pl.multiple_of(b * ROWS, ROWS), ROWS), :]
        return rows.at[pl.ds(pl.multiple_of(b * ROWS + h * (ROWS // 2), ROWS // 2), ROWS // 2), :]

    load3 = pltpu.make_async_copy(kvw.at[:, cols], kv_at(t), lsem.at[2])
    load4 = pltpu.make_async_copy(q, qg.at[z, y], lsem.at[3])
    load3.start()
    load4.start()
    load2.start()
    load1.start()

    def sec(zz, yy):
        return to_section(zz * 4 + yy)

    barrier = pltpu.get_barrier_semaphore()
    neighbours = (to_tp(mate), to_tp(xr), to_tp(xl), sec(z, yn), sec(z, yp), sec(zn, y), sec(zp, y))
    for who in neighbours:
        pl.semaphore_signal(barrier, inc=1, device_id=who, device_id_type=pl.DeviceIdType.MESH)

    for b in range(KIN // VIT):
        span = pl.ds(b * VIT, VIT)
        block = patch[:, span].astype(F32)
        centered = block - jnp.mean(block, axis=-1, keepdims=True)
        variance = jnp.mean(centered * centered, axis=-1, keepdims=True)
        rows[pl.ds(pl.multiple_of(t * ROWS, ROWS), ROWS), span] = (
            centered * lax.rsqrt(variance + 1e-06)
        ).astype(BF16)

    load3.wait()
    load4.wait()
    pl.semaphore_wait(barrier, len(neighbours))

    class Ring:
        def __init__(self, at):
            self.at = at
            self.base = recvs.take(10)

        def open(self, own):
            b = self.base
            start(own(0), self.at(t, 0), b + 0, to_tp(xr))
            start(own(1), self.at(t, 1), b + 3, to_tp(xl))
            start(own(1), self.at(t, 1), b + 1, to_tp(xr))
            start(own(0), self.at(t, 0), b + 2, to_tp(xl))
            start(own(None), self.at(t), b + 6, to_tp(mate))

        def forward(self):
            b = self.base
            arrive(self.at(xl, 0), b + 0)
            start(self.at(xl, 0), self.at(xl, 0), b + 4, to_tp(xr))
            arrive(self.at(xr, 1), b + 3)
            start(self.at(xr, 1), self.at(xr, 1), b + 5, to_tp(xl))

        def near(self):
            b = self.base
            arrive(self.at(xl, 1), b + 1)
            start(self.at(xl), self.at(xl), b + 7, to_tp(mate))
            arrive(self.at(xr, 0), b + 2)
            start(self.at(xr), self.at(xr), b + 8, to_tp(mate))

        def far(self):
            b = self.base
            arrive(self.at(xo, 0), b + 4)
            arrive(self.at(xo, 1), b + 5)
            start(self.at(xo), self.at(xo), b + 9, to_tp(mate))

        def mates(self, k):
            chip = (x, cl, cr, co)[k]
            arrive(self.at(2 * chip + (1 - c)), self.base + 6 + k)

    kv_ring = Ring(kv_at)
    kv_ring.open(lambda h: kv_at(t, h))

    class Cross:
        def __init__(self, at, me, nxt, prv, opp, dev_n, dev_p, r0, half):
            self.at, self.me, self.nxt, self.prv, self.opp = at, me, nxt, prv, opp
            self.dev_n, self.dev_p, self.r0, self.half = dev_n, dev_p, r0, half
            self.base = recvs.take(6)

        def low(self, k):
            return self.at(k, self.r0, self.half // 2)

        def high(self, k):
            return self.at(k, self.r0 + self.half // 2, self.half // 2)

        def open(self):
            b, low, high = self.base, self.low(self.me), self.high(self.me)
            start(low, low, b + 0, self.dev_n)
            start(high, high, b + 3, self.dev_p)
            start(high, high, b + 1, self.dev_n)
            start(low, low, b + 2, self.dev_p)

        def forward(self):
            b, low, high = self.base, self.low(self.prv), self.high(self.nxt)
            arrive(low, b + 0)
            start(low, low, b + 4, self.dev_n)
            arrive(high, b + 3)
            start(high, high, b + 5, self.dev_p)

        def finish(self):
            b = self.base
            arrive(self.high(self.prv), b + 1)
            arrive(self.low(self.nxt), b + 2)
            arrive(self.low(self.opp), b + 4)
            arrive(self.high(self.opp), b + 5)

    to_y = (y, yn, yp, yo, sec(z, yn), sec(z, yp))
    to_z = (z, zn, zp, zo, sec(zn, y), sec(zp, y))

    qy_first = Cross(lambda yy, r, n: qg.at[z, yy, :, pl.ds(r, n)], *to_y, 0, 512)
    qz_first = Cross(lambda zz, r, n: qg.at[zz, y, :, pl.ds(r, n)], *to_z, 512, 512)
    qz_then = Cross(lambda zz, r, n: qg.at[zz, :, :, pl.ds(r, n)], *to_z, 0, 512)
    qy_then = Cross(lambda yy, r, n: qg.at[:, yy, :, pl.ds(r, n)], *to_y, 512, 512)
    qy_first.open()
    qz_first.open()

    def w_step(b, first=False):
        part = jnp.dot(
            w2v[:, pl.ds(pl.multiple_of(b * KVB, KVB), KVB)],
            kvg[pl.ds(pl.multiple_of(b * KVB, KVB), KVB), :],
            preferred_element_type=F32,
        )
        if first:
            wacc[...] = part
        else:
            wacc[...] += part

    load2.wait()
    w_step(t, first=True)
    kv_ring.mates(0)
    w_step(mate)
    kv_ring.forward()
    row_ring = Ring(rows_at)
    row_ring.open(lambda h: rows_at(t, h))
    qy_first.forward()
    qz_first.forward()
    kv_ring.near()
    w_step(xl)
    w_step(xr)
    kv_ring.mates(1)
    w_step(2 * cl + (1 - c))
    kv_ring.mates(2)
    w_step(2 * cr + (1 - c))
    qy_first.finish()
    qz_first.finish()
    qz_then.open()
    qy_then.open()
    kv_ring.far()
    w_step(xo)
    kv_ring.mates(3)
    w_step(2 * co + (1 - c))

    def lanes(yy):
        return pl.ds(pl.multiple_of((yy % 2) * HD, HD), HD)

    def block_at(zz, yy, r0, n):
        return wg.at[zz, yy // 2, pl.ds(r0, n), lanes(yy)]

    def line_at(zz, r0, n):
        return wg.at[zz, :, pl.ds(r0, n), :]

    def column_at(yy, r0, n):
        return wg.at[:, yy // 2, pl.ds(r0, n), lanes(yy)]

    wg[z, y // 2, :, lanes(y)] = wacc[...].astype(BF16)

    y_first = Cross(lambda yy, r, n: block_at(z, yy, r, n), *to_y, 0, HALF)
    z_first = Cross(lambda zz, r, n: block_at(zz, y, r, n), *to_z, HALF, HALF)
    z_then = Cross(line_at, *to_z, 0, HALF)
    y_then = Cross(column_at, *to_y, HALF, HALF)
    y_first.open()
    z_first.open()

    def hidden(g):
        r = pl.ds(pl.multiple_of(g * GROUP, GROUP), GROUP)

        def part(k):
            span = pl.ds(pl.multiple_of(k * 1024, 1024), 1024)
            return jnp.dot(rows[r, span], w1v[span, :], preferred_element_type=F32)

        hacc[...] = part(0)

        @pl.loop(1, KIN // 1024)
        def _(k):
            hacc[...] += part(k)

        pre = hacc[...]
        hidb[g] = (0.5 * pre * (1.0 + lax.erf(pre * np.float32(math.sqrt(0.5))))).astype(BF16)

    p_base = recvs.take(4)
    p_send = sends.take(4)

    def pair_copy(k, g):
        return pltpu.make_async_remote_copy(
            src_ref=psend.at[g], dst_ref=precv.at[g], send_sem=ssem.at[p_send + k],
            recv_sem=rsem.at[p_base + k], device_id=to_tp(mate), device_id_type=pl.DeviceIdType.MESH,
        )

    def project(k, g):
        hid = hidb[g]
        for xx in range(4):
            psend[g, xx] = jnp.dot(hid, wg[xx, 1 - c], preferred_element_type=F32).astype(BF16)
        pair_copy(k, g).start()
        for xx in range(4):
            mine[g, xx] = jnp.dot(hid, wg[xx, c], preferred_element_type=F32)

    h1_base = recvs.take(8)
    h1_send = sends.take(8)
    h2_base = recvs.take(8)
    h2_send = sends.take(8)

    def hop(src, dst, ssl, rsl, way, g):
        return pltpu.make_async_remote_copy(
            src_ref=src.at[way, g], dst_ref=dst.at[way, g], send_sem=ssem.at[ssl + way * 4 + g],
            recv_sem=rsem.at[rsl + way * 4 + g], device_id=to_tp((xr, xl)[way]),
            device_id_type=pl.DeviceIdType.MESH,
        )

    def hop1(way, g):
        return hop(h1s, h1r, h1_send, h1_base, way, g)

    def hop2(way, g):
        return hop(h2s, h2r, h2_send, h2_base, way, g)

    def pair_sum(k, g):
        pair_copy(k, g).wait_recv()
        for xx in range(4):
            mine[g, xx] += precv[g, xx].astype(F32)
        for way in range(2):
            h1s[way, g] = mine[g, co, way * ROWS : (way + 1) * ROWS, :].astype(BF16)
            hop1(way, g).start()

    def middle(way, g):
        hop1(way, g).wait_recv()
        dest = (cr, cl)[way]
        near, other = way * ROWS, (1 - way) * ROWS
        h2s[way, g, near : near + ROWS, :] = (
            mine[g, dest, near : near + ROWS, :] + h1r[way, g].astype(F32)
        ).astype(BF16)
        h2s[way, g, other : other + ROWS, :] = mine[g, dest, other : other + ROWS, :].astype(BF16)
        hop2(way, g).start()

    def last(g):
        hop2(0, g).wait_recv()
        hop2(1, g).wait_recv()
        total = mine[g, x] + h2r[0, g].astype(F32) + h2r[1, g].astype(F32)
        key = total[:, :HD]
        r = pl.ds(pl.multiple_of(g * GROUP, GROUP), GROUP)
        place = pl.ds(pl.multiple_of((g % 2) * GROUP, GROUP), GROUP)
        kbuf[r, :] = (key * ktab[0, place, :] + pltpu.roll(key, HD // 2, 1) * ktab[1, place, :]).astype(BF16)
        vt[:, r] = total[:, HD:].T.astype(BF16)

    lane = lax.broadcasted_iota(jnp.int32, (HD, HD), 1)
    sub = lax.broadcasted_iota(jnp.int32, (HD, HD), 0)
    eye = lane == sub

    def column(row):
        return jnp.sum(jnp.where(eye, row.astype(F32), 0.0), axis=1, keepdims=True)

    def heads_down(block):
        return jnp.concatenate([block[:, h * HD : (h + 1) * HD] for h in range(8)], axis=0)

    def prepare():
        counts = lens[...]
        code = jnp.zeros((1, HD), jnp.int32)
        for j in range(CITE):
            cited = cites[j : j + 1, :]
            hit = (counts > j) & ((cited // 2) == s)
            code += jnp.where(hit, 1 + (cited % 2) + 2 * (counts - 1 - j), 0)
        code = column(code)
        owned = column(prefills[...]) == (lane % NS).astype(F32)
        decode = column(decodes[...])
        codeb[NS] = jnp.sum(
            jnp.where(owned & (decode == s.astype(F32)), 1.0, 0.0), axis=0, keepdims=True
        )

        @pl.loop(0, NS)
        def _(i):
            d = (s + i) % NS
            row = jnp.sum(jnp.where(owned & (decode == d.astype(F32)), code, 0.0), axis=0, keepdims=True)
            codeb[i] = row
            col = column(row)
            cosine, sine = qtab[0, 0:1, :], qtab[1, 0:1, :]
            for p in range(1, CITE):
                now = (col == 1.0 + 2.0 * p) | (col == 2.0 + 2.0 * p)
                cosine = jnp.where(now, qtab[0, p : p + 1, :], cosine)
                sine = jnp.where(now, qtab[1, p : p + 1, :], sine)
            asks = heads_down(qg[d // 4, d % 4].astype(F32))
            askb[i] = (asks * cosine + pltpu.roll(asks, HD // 2, 1) * sine).astype(BF16)

    load1.wait()
    row_ring.mates(0)
    hidden(x)
    y_first.forward()
    z_first.forward()
    qz_then.forward()
    qy_then.forward()
    row_ring.forward()
    y_first.finish()
    z_first.finish()
    z_then.open()
    y_then.open()
    qz_then.finish()
    qy_then.finish()
    prepare()
    z_then.forward()
    y_then.forward()
    row_ring.near()
    row_ring.mates(1)
    hidden(cl)
    row_ring.mates(2)
    hidden(cr)
    z_then.finish()
    y_then.finish()
    project(0, x)
    project(1, cl)
    pair_sum(0, x)
    project(2, cr)
    pair_sum(1, cl)
    row_ring.far()
    pair_sum(2, cr)
    row_ring.mates(3)
    hidden(co)
    middle(0, x)
    middle(1, x)
    middle(0, cl)
    middle(1, cr)
    project(3, co)
    pair_sum(3, co)
    middle(0, cr)
    middle(1, cl)
    middle(0, co)
    middle(1, co)
    order = (x, cl, cr, co)
    for g in order:
        last(g)

    inv_root = np.float32(1.0 / math.sqrt(HD))
    o_base = recvs.take(NS)
    o_send = sends.take(NS)

    def part_of(i):
        asks = askb[pl.ds(i, 2)].reshape(2 * HD, HD)
        row = jnp.concatenate([codeb[i], codeb[i + 1]], axis=1)
        scores = lax.dot_general(kbuf[...], asks, (((1,), (1,)), ((), ())), preferred_element_type=F32)
        second = (row == 2.0) | (row == 4.0) | (row == 6.0) | (row == 8.0)
        frame = jnp.where(second, scores[256:], scores[:256]) * inv_root
        top = jnp.max(frame, axis=0, keepdims=True)
        weight = jnp.exp(frame - top)
        total = jnp.sum(weight, axis=0, keepdims=True)
        both = jnp.concatenate([jnp.where(second, 0.0, weight), jnp.where(second, weight, 0.0)], axis=0)
        value = jnp.dot(vt[...], both.astype(BF16), preferred_element_type=F32) / total
        live = row > 0.0
        value = jnp.where(live, value, 0.0).astype(BF16)
        level = jnp.where(live, top + jnp.log(total), -1e30)
        high = level.astype(BF16).astype(F32)
        mid = (level - high).astype(BF16).astype(F32)
        low = level - high - mid
        pad = jnp.zeros((PART - HD - 3, 2 * HD), F32)
        level = jnp.concatenate([high, mid, low, pad], axis=0).astype(BF16)
        for k in range(2):
            d = (s + i + k) % NS
            osend[d, 0:HD, :] = value[:, k * HD : (k + 1) * HD]
            osend[d, HD:PART, :] = level[:, k * HD : (k + 1) * HD]

    def part_copy(i):
        d = (s + i) % NS
        return pltpu.make_async_remote_copy(
            src_ref=osend.at[d], dst_ref=orecv.at[s], send_sem=ssem.at[o_send + i],
            recv_sem=rsem.at[o_base + i], device_id=to_section(d), device_id_type=pl.DeviceIdType.MESH,
        )

    @pl.loop(1, NS // 2)
    def _(i):
        part_of(2 * i)
        part_copy(2 * i).start()
        part_copy(2 * i + 1).start()

    part_of(0)
    part_copy(1).start()
    keep = pltpu.make_async_copy(osend.at[s], orecv.at[s], lsem.at[4])
    keep.start()

    asks = heads_down(q[...].astype(F32)).astype(BF16)
    own = lax.dot_general(nkv[:, :HD], asks, (((1,), (1,)), ((), ())), preferred_element_type=F32)
    pick = (lax.broadcasted_iota(jnp.int32, (NS, HD), 1) % NS) == lax.broadcasted_iota(jnp.int32, (NS, HD), 0)
    own = jnp.sum(jnp.where(pick, own, 0.0), axis=0, keepdims=True) * inv_root
    value = nkv[:, HD:].astype(F32)
    value = jnp.concatenate([value] * 8, axis=0).T
    present = codeb[NS]

    keep.wait()

    @pl.loop(1, NS)
    def _(i):
        part_copy(i).wait_recv()

    tail = [orecv[j, HD:PART, :].astype(F32) for j in range(NS)]
    level = [v[0:1] + v[1:2] + v[2:3] for v in tail]
    top = own
    for v in level:
        top = jnp.maximum(top, v)
    weight = jnp.exp(own - top)
    total, value = weight, value * weight
    for j in range(NS):
        weight = jnp.exp(level[j] - top)
        total += weight
        value += orecv[j, 0:HD, :].astype(F32) * weight
    value = jnp.where(present > 0.0, value / total, 0.0).T
    for h in range(8):
        out[:, h * HD : (h + 1) * HD] = value[h * NS : (h + 1) * NS, :].astype(BF16)

    for copy in pending:
        copy.wait_send()
    for k, g in enumerate(order):
        pair_copy(k, g).wait_send()
        for way in range(2):
            hop1(way, g).wait_send()
            hop2(way, g).wait_send()

    @pl.loop(1, NS)
    def _(i):
        part_copy(i).wait_send()

    assert (sends.n, recvs.n) == (N_SEND, N_RECV), (sends.n, recvs.n)


def shards(
    patch_states, merge_in, merge_out, kv_weight, queries, new_kv, citations, lengths, prefill_owner, decode_owner
):
    along = (1, citations.shape[0])
    keys, asks = tables()
    vmem = pl.BlockSpec(memory_space=pltpu.VMEM)
    anywhere = pl.BlockSpec(memory_space=pl.ANY)
    result = pl.pallas_call(
        kernel,
        out_shape=jax.ShapeDtypeStruct((NS, 8 * HD), BF16),
        in_specs=[vmem, anywhere, anywhere, anywhere] + [vmem] * 8,
        out_specs=vmem,
        scratch_shapes=[
            pltpu.VMEM((TOKENS, KIN), BF16),
            pltpu.VMEM((KIN, HU), BF16),
            pltpu.VMEM((HU, 8192), BF16),
            pltpu.VMEM((8192, HD), BF16),
            pltpu.VMEM((HU, HD), F32),
            pltpu.VMEM((4, 2, HU, 2 * HD), BF16),
            pltpu.VMEM((GROUP, HU), F32),
            pltpu.VMEM((4, GROUP, HU), BF16),
            pltpu.VMEM((4, 4, GROUP, 2 * HD), F32),
            pltpu.VMEM((4, 4, GROUP, 2 * HD), BF16),
            pltpu.VMEM((4, 4, GROUP, 2 * HD), BF16),
            pltpu.VMEM((2, 4, ROWS, 2 * HD), BF16),
            pltpu.VMEM((2, 4, ROWS, 2 * HD), BF16),
            pltpu.VMEM((2, 4, GROUP, 2 * HD), BF16),
            pltpu.VMEM((2, 4, GROUP, 2 * HD), BF16),
            pltpu.VMEM((TOKENS, HD), BF16),
            pltpu.VMEM((HD, TOKENS), BF16),
            pltpu.VMEM((4, 4, NS, 8 * HD), BF16),
            pltpu.VMEM((NS, HD, HD), BF16),
            pltpu.VMEM((NS + 1, 1, HD), F32),
            pltpu.VMEM((NS, PART, HD), BF16),
            pltpu.VMEM((NS, PART, HD), BF16),
            pltpu.SemaphoreType.DMA((N_SEND,)),
            pltpu.SemaphoreType.DMA((N_RECV,)),
            pltpu.SemaphoreType.DMA((N_LOCAL,)),
        ],
        compiler_params=pltpu.CompilerParams(
            collective_id=0, has_side_effects=True, vmem_limit_bytes=58 * 1024 * 1024
        ),
    )(
        patch_states, merge_in, merge_out, kv_weight, queries[0], new_kv[0],
        citations.T, lengths.reshape(along), prefill_owner.reshape(along), decode_owner.reshape(along),
        jnp.asarray(keys), jnp.asarray(asks),
    )
    return result[None]


def solution(mesh):
    return jax.shard_map(
        shards,
        mesh=mesh,
        in_specs=(
            P(("section", "tp"), None),
            P(None, "tp"),
            P("tp", None),
            P("tp", None),
            P("section", None, "tp"),
            P("section", None, "tp"),
            P(),
            P(),
            P(),
            P(),
        ),
        out_specs=P("section", None, "tp"),
        check_vma=False,
    )
```

```python
import math

import jax
import jax.numpy as jnp
import numpy as np
from jax import lax
from jax.experimental import pallas as pl
from jax.experimental.pallas import tpu as pltpu
from jax.sharding import PartitionSpec as P

F32 = jnp.float32
BF16 = jnp.bfloat16
VIT = 1280
HD = 128
GRID = 16
NS = 16
CITE = 4
ROWS = 64
GROUP = 128
TOKENS = 512
KIN = 5120
HU = 640
CHUNK = 1024
KVB = 1024
HALF = HU // 2
QUARTER = HU // 4


def tables():
    slot = np.arange(HD // 2)
    inverse = np.exp(slot.astype(np.float32) * np.float32(-2.0 * math.log(1000000.0) / HD)).astype(np.float32)
    token = np.arange(GRID * GRID)
    height = (token // GRID).astype(np.float32)
    across = (token % GRID).astype(np.float32)
    first = HD // 8
    second = first + 3 * HD // 16
    spatial = np.where(slot[None, :] < second, height[:, None], across[:, None])
    spatial = np.where(slot[None, :] < first, np.float32(0.0), spatial) * inverse[None, :]
    cosine, sine = np.cos(spatial), np.sin(spatial)
    keys = np.stack([np.concatenate([cosine, cosine], 1), np.concatenate([-sine, sine], 1)])
    steps = np.arange(CITE).astype(np.float32)[:, None] * inverse[None, :]
    steps = np.where(slot[None, :] < first, steps, np.float32(0.0))
    cosine, sine = np.cos(steps), np.sin(steps)
    asks = np.stack([np.concatenate([cosine, cosine], 1), np.concatenate([sine, -sine], 1)])
    return keys.astype(np.float32), asks.astype(np.float32)


class Counter:
    def __init__(self):
        self.n = 0

    def take(self, k=1):
        first = self.n
        self.n += k
        return first


N_SEND = 10
N_RECV = 110
N_LOCAL = 7


def kernel(
    patch_in, w1, w2, kvw, q, nkv, cites, lens, prefills, decodes, ktab_in, qtab, out,
    patch, ktab, rows, w1v, w2v, kvg, wacc, wg, hacc, hidb, mine, psend, precv, gsend, grecv,
    kbuf, vt, qg, askb, codeb, osend, orecv, lsend, lrecv, ssem, rsem, lsem,
):
    s = lax.axis_index("section")
    t = lax.axis_index("tp")
    x, c = t // 2, t % 2
    z, y = s // 4, s % 4
    mate = 2 * x + (1 - c)
    cr, cl, co = (x + 1) % 4, (x + 3) % 4, (x + 2) % 4
    xr, xl, xo = 2 * cr + c, 2 * cl + c, 2 * co + c
    yn, yp, yo = (y + 1) % 4, (y + 3) % 4, (y + 2) % 4
    zn, zp, zo = (z + 1) % 4, (z + 3) % 4, (z + 2) % 4
    recvs = Counter()
    kv_out, row_out, q_out, q_out_then, a_out, b_out, p_out, g_out, o_out, l_out = range(10)

    def to_tp(who):
        return {"tp": who}

    def to_section(who):
        return {"section": who}

    def remote(src, dst, kind, slot, dev):
        return pltpu.make_async_remote_copy(
            src_ref=src, dst_ref=dst, send_sem=ssem.at[kind], recv_sem=rsem.at[slot],
            device_id=dev, device_id_type=pl.DeviceIdType.MESH,
        )

    def start(src, dst, kind, slot, dev):
        remote(src, dst, kind, slot, dev).start()

    def arrive(dst, slot):
        remote(dst, dst, 0, slot, to_tp(mate)).wait_recv()

    def sent(kind, ref):
        remote(ref, ref, kind, 0, to_tp(mate)).wait_send()

    def sec(zz, yy):
        return to_section(zz * 4 + yy)

    barrier = pltpu.get_barrier_semaphore()
    neighbours = (to_tp(mate), to_tp(xr), to_tp(xl), sec(z, yn), sec(z, yp), sec(zn, y), sec(zp, y))
    for who in neighbours:
        pl.semaphore_signal(barrier, inc=1, device_id=who, device_id_type=pl.DeviceIdType.MESH)

    load1 = pltpu.make_async_copy(w1, w1v, lsem.at[0])
    load2 = pltpu.make_async_copy(w2, w2v, lsem.at[1])
    cols = pl.ds(pl.multiple_of(s * HD, HD), HD)

    def kv_at(b, h=None):
        if h is None:
            return kvg.at[pl.ds(pl.multiple_of(b * KVB, KVB), KVB), :]
        return kvg.at[pl.ds(pl.multiple_of(b * KVB + h * (KVB // 2), KVB // 2), KVB // 2), :]

    def rows_at(b, h=None):
        if h is None:
            return rows.at[pl.ds(pl.multiple_of(b * ROWS, ROWS), ROWS), :]
        return rows.at[pl.ds(pl.multiple_of(b * ROWS + h * (ROWS // 2), ROWS // 2), ROWS // 2), :]

    load3 = pltpu.make_async_copy(kvw.at[:, cols], kv_at(t), lsem.at[2])
    load4 = pltpu.make_async_copy(q, qg.at[z, y], lsem.at[3])
    load5 = pltpu.make_async_copy(patch_in, patch, lsem.at[5])
    load6 = pltpu.make_async_copy(ktab_in, ktab, lsem.at[6])
    load3.start()
    load4.start()
    load5.start()
    load2.start()
    load1.start()
    load6.start()

    load3.wait()
    pl.semaphore_wait(barrier, len(neighbours))

    class Ring:
        def __init__(self, at, kind):
            self.at, self.kind = at, kind
            self.base = recvs.take(10)

        def go(self, *rest):
            start(*rest[:2], self.kind, *rest[2:])

        def open(self, own):
            b = self.base
            self.go(own(0), self.at(t, 0), b + 0, to_tp(xr))
            self.go(own(1), self.at(t, 1), b + 3, to_tp(xl))
            self.go(own(1), self.at(t, 1), b + 1, to_tp(xr))
            self.go(own(0), self.at(t, 0), b + 2, to_tp(xl))
            self.go(own(None), self.at(t), b + 6, to_tp(mate))

        def forward(self):
            b = self.base
            arrive(self.at(xl, 0), b + 0)
            self.go(self.at(xl, 0), self.at(xl, 0), b + 4, to_tp(xr))
            arrive(self.at(xr, 1), b + 3)
            self.go(self.at(xr, 1), self.at(xr, 1), b + 5, to_tp(xl))

        def near(self):
            b = self.base
            arrive(self.at(xl, 1), b + 1)
            self.go(self.at(xl), self.at(xl), b + 7, to_tp(mate))
            arrive(self.at(xr, 0), b + 2)
            self.go(self.at(xr), self.at(xr), b + 8, to_tp(mate))

        def far(self):
            b = self.base
            arrive(self.at(xo, 0), b + 4)
            arrive(self.at(xo, 1), b + 5)
            self.go(self.at(xo), self.at(xo), b + 9, to_tp(mate))

        def mates(self, k):
            chip = (x, cl, cr, co)[k]
            arrive(self.at(2 * chip + (1 - c)), self.base + 6 + k)

    kv_ring = Ring(kv_at, kv_out)
    kv_ring.open(lambda h: kv_at(t, h))

    class Cross:
        def __init__(self, at, me, nxt, prv, opp, dev_n, dev_p, r0, half, kind):
            self.at, self.me, self.nxt, self.prv, self.opp = at, me, nxt, prv, opp
            self.dev_n, self.dev_p, self.r0, self.half, self.kind = dev_n, dev_p, r0, half, kind
            self.base = recvs.take(4)

        def low(self, k):
            return self.at(k, self.r0, self.half // 2)

        def high(self, k):
            return self.at(k, self.r0 + self.half // 2, self.half // 2)

        def open(self):
            own = self.at(self.me, self.r0, self.half)
            start(own, own, self.kind, self.base, self.dev_n)
            start(own, own, self.kind, self.base + 1, self.dev_p)

        def forward(self):
            b, low, high = self.base, self.low(self.prv), self.high(self.nxt)
            arrive(self.at(self.prv, self.r0, self.half), b)
            start(low, low, self.kind, b + 2, self.dev_n)
            arrive(self.at(self.nxt, self.r0, self.half), b + 1)
            start(high, high, self.kind, b + 3, self.dev_p)

        def finish(self):
            arrive(self.low(self.opp), self.base + 2)
            arrive(self.high(self.opp), self.base + 3)

    to_y = (y, yn, yp, yo, sec(z, yn), sec(z, yp))
    to_z = (z, zn, zp, zo, sec(zn, y), sec(zp, y))

    qy_first = Cross(lambda yy, r, n: qg.at[z, yy, :, pl.ds(r, n)], *to_y, 0, 512, q_out)
    qz_first = Cross(lambda zz, r, n: qg.at[zz, y, :, pl.ds(r, n)], *to_z, 512, 512, q_out)
    qz_then = Cross(lambda zz, r, n: qg.at[zz, :, :, pl.ds(r, n)], *to_z, 0, 512, q_out_then)
    qy_then = Cross(lambda yy, r, n: qg.at[:, yy, :, pl.ds(r, n)], *to_y, 512, 512, q_out_then)
    load4.wait()
    qy_first.open()
    qz_first.open()

    load5.wait()
    for b in range(KIN // VIT):
        span = pl.ds(b * VIT, VIT)
        block = patch[:, span].astype(F32)
        centered = block - jnp.mean(block, axis=-1, keepdims=True)
        variance = jnp.mean(centered * centered, axis=-1, keepdims=True)
        rows[pl.ds(pl.multiple_of(t * ROWS, ROWS), ROWS), span] = (
            centered * lax.rsqrt(variance + 1e-06)
        ).astype(BF16)

    lane = lax.broadcasted_iota(jnp.int32, (HD, HD), 1)
    sub = lax.broadcasted_iota(jnp.int32, (HD, HD), 0)
    eye = lane == sub

    def column(row):
        return jnp.sum(jnp.where(eye, row.astype(F32), 0.0), axis=1, keepdims=True)

    def heads_down(block):
        return jnp.concatenate([block[:, h * HD : (h + 1) * HD] for h in range(8)], axis=0)

    def windows():
        counts = lens[...]
        code = jnp.zeros((1, HD), jnp.int32)
        for j in range(CITE):
            cited = cites[j : j + 1, :]
            hit = (counts > j) & ((cited // 2) == s)
            code += jnp.where(hit, 1 + (cited % 2) + 2 * (counts - 1 - j), 0)
        code = column(code)
        owned = column(prefills[...]) == (lane % NS).astype(F32)
        decode = column(decodes[...])
        codeb[NS] = jnp.sum(
            jnp.where(owned & (decode == s.astype(F32)), 1.0, 0.0), axis=0, keepdims=True
        )

        @pl.loop(0, NS)
        def _(i):
            d = ((z + i // 4) % 4) * 4 + (y + i % 4) % 4
            row = jnp.sum(jnp.where(owned & (decode == d.astype(F32)), code, 0.0), axis=0, keepdims=True)
            codeb[i] = row

    def prepare():
        @pl.loop(0, NS)
        def _(i):
            col = column(codeb[i])
            cosine, sine = qtab[0, 0:1, :], qtab[1, 0:1, :]
            for p in range(1, CITE):
                now = (col == 1.0 + 2.0 * p) | (col == 2.0 + 2.0 * p)
                cosine = jnp.where(now, qtab[0, p : p + 1, :], cosine)
                sine = jnp.where(now, qtab[1, p : p + 1, :], sine)
            asks = heads_down(qg[(z + i // 4) % 4, (y + i % 4) % 4].astype(F32))
            askb[i] = (asks * cosine + pltpu.roll(asks, HD // 2, 1) * sine).astype(BF16)

    windows()

    def w_step(b, first=False):
        part = jnp.dot(
            w2v[:, pl.ds(pl.multiple_of(b * KVB, KVB), KVB)],
            kvg[pl.ds(pl.multiple_of(b * KVB, KVB), KVB), :],
            preferred_element_type=F32,
        )
        if first:
            wacc[...] = part
        else:
            wacc[...] += part

    load2.wait()
    w_step(t, first=True)
    kv_ring.mates(0)
    w_step(mate)
    kv_ring.forward()
    row_ring = Ring(rows_at, row_out)
    row_ring.open(lambda h: rows_at(t, h))
    qy_first.forward()
    qz_first.forward()
    kv_ring.near()
    w_step(xl)
    w_step(xr)
    kv_ring.mates(1)
    w_step(2 * cl + (1 - c))
    kv_ring.mates(2)
    w_step(2 * cr + (1 - c))
    qy_first.finish()
    qz_first.finish()
    qz_then.open()
    qy_then.open()
    kv_ring.far()
    w_step(xo)
    kv_ring.mates(3)
    w_step(2 * co + (1 - c))

    def lanes(yy):
        return pl.ds(pl.multiple_of((yy % 2) * HD, HD), HD)

    def block_at(zz, yy, r0, n):
        return wg.at[zz, yy // 2, pl.ds(r0, n), lanes(yy)]

    wg[z, y // 2, :, lanes(y)] = wacc[...].astype(BF16)

    class Spread:
        def __init__(self, at, first, second, kind):
            self.at, self.kind = at, kind
            self.p, self.pn, self.pp, self.po, self.dev1n, self.dev1p = first
            self.q, self.qn, self.qp, self.qo, self.dev2n, self.dev2p = second
            self.along = (self.p, self.pp, self.pn, self.po)
            self.base = recvs.take(20)

        def whole(self, p, q):
            return self.at(p, q, 0, HALF)

        def low(self, p, q):
            return self.at(p, q, 0, QUARTER)

        def high(self, p, q):
            return self.at(p, q, QUARTER, QUARTER)

        def go(self, ref, slot, dev):
            start(ref, ref, self.kind, self.base + slot, dev)

        def across(self, k):
            block = self.whole(self.along[k], self.q)
            self.go(block, 4 + 4 * k, self.dev2n)
            self.go(block, 5 + 4 * k, self.dev2p)

        def open(self):
            block = self.whole(self.p, self.q)
            self.go(block, 0, self.dev1n)
            self.go(block, 1, self.dev1p)

        def near(self):
            arrive(self.whole(self.pp, self.q), self.base)
            self.go(self.low(self.pp, self.q), 2, self.dev1n)
            arrive(self.whole(self.pn, self.q), self.base + 1)
            self.go(self.high(self.pn, self.q), 3, self.dev1p)

        def far(self):
            arrive(self.low(self.po, self.q), self.base + 2)
            arrive(self.high(self.po, self.q), self.base + 3)
            self.across(3)

        def turn(self, k):
            p = self.along[k]
            arrive(self.whole(p, self.qp), self.base + 4 + 4 * k)
            self.go(self.low(p, self.qp), 6 + 4 * k, self.dev2n)
            arrive(self.whole(p, self.qn), self.base + 5 + 4 * k)
            self.go(self.high(p, self.qn), 7 + 4 * k, self.dev2p)

        def finish(self):
            for k in range(4):
                p = self.along[k]
                arrive(self.low(p, self.qo), self.base + 6 + 4 * k)
                arrive(self.high(p, self.qo), self.base + 7 + 4 * k)

    upper = Spread(lambda yy, zz, r, n: block_at(zz, yy, r, n), to_y, to_z, a_out)
    lower = Spread(lambda zz, yy, r, n: block_at(zz, yy, HALF + r, n), to_z, to_y, b_out)
    upper.open()
    lower.open()
    upper.across(0)
    lower.across(0)

    far_base = recvs.take(KIN // CHUNK)

    def far_part(b, k):
        return rows_at(b).at[:, pl.ds(k * CHUNK, CHUNK)]

    def far_rows():
        arrive(rows_at(xo, 0), row_ring.base + 4)
        arrive(rows_at(xo, 1), row_ring.base + 5)
        for k in range(KIN // CHUNK):
            start(far_part(xo, k), far_part(xo, k), row_out, far_base + k, to_tp(mate))

    def far_ready(k):
        arrive(far_part(2 * co + (1 - c), k), far_base + k)

    def hidden(*groups, ready=None):
        spans = [pl.ds(pl.multiple_of(g * GROUP, GROUP), GROUP) for g in groups]
        used = pl.ds(0, len(groups) * GROUP)

        def part(k):
            span = pl.ds(pl.multiple_of(k * CHUNK, CHUNK), CHUNK)
            left = jnp.concatenate([rows[r, span] for r in spans], axis=0)
            return jnp.dot(left, w1v[span, :], preferred_element_type=F32)

        if ready is None:
            hacc[used] = part(0)

            @pl.loop(1, KIN // CHUNK)
            def _(k):
                hacc[used] += part(k)
        else:
            for k in range(KIN // CHUNK):
                ready(k)
                if k == 0:
                    hacc[used] = part(k)
                else:
                    hacc[used] += part(k)

        for n, g in enumerate(groups):
            pre = hacc[n * GROUP : (n + 1) * GROUP]
            hidb[g] = (0.5 * pre * (1.0 + lax.erf(pre * np.float32(math.sqrt(0.5))))).astype(BF16)

    p_base = recvs.take(16)
    g_base = recvs.take(11)
    order = (x, cl, cr, co)
    dests = (co, cr, cl, x)

    def pair_copy(k, n):
        g = order[k]
        return remote(psend.at[g, n], precv.at[g, n], p_out, p_base + 4 * k + n, to_tp(mate))

    lower_rows, upper_rows = pl.ds(0, ROWS), pl.ds(ROWS, ROWS)
    A_R, A_L, B_R, B_L, C_L, C_R, E_R, E_L, F_R, F_L, F_O = range(11)
    places = {
        A_R: (0, lower_rows), A_L: (0, upper_rows), B_R: (1,), B_L: (2,), C_L: (pl.ds(3, 2),), C_R: (pl.ds(5, 2),),
        E_R: (7,), E_L: (8,), F_R: (9,), F_L: (10,), F_O: (11,),
    }

    def relay(m):
        who = {A_R: xr, B_R: xr, C_R: xr, E_R: xr, F_R: xr, F_O: xo}.get(m, xl)
        return remote(gsend.at[places[m]], grecv.at[places[m]], g_out, g_base + m, to_tp(who))

    def project(k):
        hid = hidb[order[k]]
        for n in range(4):
            psend[order[k], n] = jnp.dot(hid, wg[dests[n], 1 - c], preferred_element_type=F32).astype(BF16)
            pair_copy(k, n).start()
        for n in range(4):
            mine[order[k], n] = jnp.dot(hid, wg[dests[n], c], preferred_element_type=F32)

    def pair_sum(k):
        g = order[k]
        out_now = (
            {0: None},
            {0: 3, 2: 4},
            {0: 5, 1: 6},
            {0: 11, 1: 9, 2: 10},
        )[k]
        after = ({0: (A_R, A_L)}, {2: (C_L,)}, {1: (C_R,)}, {0: (F_O,), 1: (F_R,), 2: (F_L,)})[k]
        for n in range(4):
            pair_copy(k, n).wait_recv()
            total = mine[g, n] + precv[g, n].astype(F32)
            if n not in out_now:
                mine[g, n] = total
            else:
                gsend[out_now[n] or 0] = total.astype(BF16)
            for m in after.get(n, ()):
                relay(m).start()

    def pass_halves():
        relay(A_R).wait_recv()
        gsend[7, :ROWS] = (mine[cl, 1, :ROWS] + grecv[0, :ROWS].astype(F32)).astype(BF16)
        gsend[7, ROWS:] = mine[cl, 1, ROWS:].astype(BF16)
        relay(E_R).start()
        relay(A_L).wait_recv()
        gsend[8, :ROWS] = mine[cr, 2, :ROWS].astype(BF16)
        gsend[8, ROWS:] = (mine[cr, 2, ROWS:] + grecv[0, ROWS:].astype(F32)).astype(BF16)
        relay(E_L).start()

    def pass_on():
        relay(C_R).wait_recv()
        gsend[1] = (mine[x, 1] + grecv[5].astype(F32)).astype(BF16)
        relay(B_R).start()
        relay(C_L).wait_recv()
        gsend[2] = (mine[x, 2] + grecv[3].astype(F32)).astype(BF16)
        relay(B_L).start()

    def last(k):
        g = order[k]
        total = mine[g, 3]
        for m, n in (((F_O, 11), (None, 4), (None, 6)), ((B_R, 1), (F_L, 10)), ((B_L, 2), (F_R, 9)), ((E_R, 7), (E_L, 8)))[k]:
            if m is not None:
                relay(m).wait_recv()
            total += grecv[n].astype(F32)
        key = total[:, :HD]
        r = pl.ds(pl.multiple_of(g * GROUP, GROUP), GROUP)
        place = pl.ds(pl.multiple_of((g % 2) * GROUP, GROUP), GROUP)
        kbuf[r, :] = (key * ktab[0, place, :] + pltpu.roll(key, HD // 2, 1) * ktab[1, place, :]).astype(BF16)
        vt[:, r] = total[:, HD:].T.astype(BF16)

    load1.wait()
    row_ring.mates(0)
    hidden(x)
    upper.near()
    lower.near()
    for k in (1, 2):
        upper.across(k)
        lower.across(k)
    upper.turn(0)
    lower.turn(0)
    upper.far()
    lower.far()
    row_ring.forward()
    upper.turn(1)
    lower.turn(1)
    upper.turn(2)
    lower.turn(2)
    qz_then.forward()
    qy_then.forward()
    row_ring.near()
    upper.turn(3)
    lower.turn(3)
    row_ring.mates(1)
    row_ring.mates(2)
    hidden(cl, cr)
    qz_then.finish()
    qy_then.finish()
    upper.finish()
    lower.finish()
    project(0)
    project(1)
    pair_sum(0)
    project(2)
    pair_sum(1)
    far_rows()
    pair_sum(2)
    pass_halves()
    hidden(co, ready=far_ready)
    project(3)
    pass_on()
    pair_sum(3)
    prepare()
    load6.wait()
    for k in (1, 2, 3, 0):
        last(k)

    inv_root = np.float32(1.0 / math.sqrt(HD))
    o_base = recvs.take(2)

    def place(i):
        return ((z + i // 4) % 4) * 4 + (y + i % 4) % 4

    def scores_of(sections):
        asks = jnp.concatenate([askb[i] for i in sections], axis=0)
        return lax.dot_general(kbuf[...], asks, (((1,), (1,)), ((), ())), preferred_element_type=F32)

    def part_of(sections, scores):
        row = jnp.concatenate([codeb[i] for i in sections], axis=1)
        second = (row == 2.0) | (row == 4.0) | (row == 6.0) | (row == 8.0)
        frame = jnp.where(second, scores[256:], scores[:256]) * inv_root
        top = jnp.max(frame, axis=0, keepdims=True)
        weight = jnp.exp(frame - top)
        total = jnp.sum(weight, axis=0, keepdims=True)
        both = jnp.concatenate([jnp.where(second, 0.0, weight), jnp.where(second, weight, 0.0)], axis=0)
        value = jnp.dot(vt[...], both.astype(BF16), preferred_element_type=F32) / total
        live = row > 0.0
        value = jnp.where(live, value, 0.0).astype(BF16)
        level = jnp.where(live, top + jnp.log(total), -1e30)
        for k, i in enumerate(sections):
            osend[place(i)] = value[:, k * HD : (k + 1) * HD]
            lsend[place(i)] = level[:, k * HD : (k + 1) * HD]

    def part_copies(i):
        d = place(i)
        who = to_section(d)
        return (
            remote(lsend.at[d], lrecv.at[s], l_out, o_base + 1, who),
            remote(osend.at[d], orecv.at[s], o_out, o_base, who),
        )

    turns = ((10, 9, 11, 6), (14, 5, 15, 7), (13, 8, 2, 4), (12, 1, 3, 0))
    scores = scores_of(turns[0])
    for n, sections in enumerate(turns):
        now = scores
        if n + 1 < len(turns):
            scores = scores_of(turns[n + 1])
        part_of(sections, now)
        for i in sections:
            if i > 0:
                for copy in part_copies(i):
                    copy.start()
    orecv[s] = osend[s]
    lrecv[s] = lsend[s]

    asks = heads_down(q[...].astype(F32)).astype(BF16)
    own = lax.dot_general(nkv[:, :HD], asks, (((1,), (1,)), ((), ())), preferred_element_type=F32)
    pick = (lax.broadcasted_iota(jnp.int32, (NS, HD), 1) % NS) == lax.broadcasted_iota(jnp.int32, (NS, HD), 0)
    own = jnp.sum(jnp.where(pick, own, 0.0), axis=0, keepdims=True) * inv_root
    value = nkv[:, HD:].astype(F32)
    value = jnp.concatenate([value] * 8, axis=0).T
    present = codeb[NS]

    arrive(lrecv.at[pl.ds(0, NS - 1)], o_base + 1)
    arrive(orecv.at[pl.ds(0, NS - 1)], o_base)

    level = [lrecv[j] for j in range(NS)]
    top = own
    for v in level:
        top = jnp.maximum(top, v)
    weight = jnp.exp(own - top)
    total, value = weight, value * weight
    for j in range(NS):
        weight = jnp.exp(level[j] - top)
        total += weight
        value += orecv[j].astype(F32) * weight
    value = jnp.where(present > 0.0, value / total, 0.0).T
    for h in range(8):
        out[:, h * HD : (h + 1) * HD] = value[h * NS : (h + 1) * NS, :].astype(BF16)

    units = 15 * HALF
    sent(kv_out, kvg.at[pl.ds(0, 7 * KVB), :])
    sent(row_out, rows.at[pl.ds(0, 7 * ROWS), :])
    sent(q_out, qg.at[0, pl.ds(0, 3)])
    sent(q_out_then, qg.at[pl.ds(0, 3)])
    sent(a_out, kvg.at[pl.ds(0, units), :])
    sent(b_out, kvg.at[pl.ds(0, units), :])
    sent(p_out, psend)
    sent(g_out, gsend)
    sent(o_out, osend.at[pl.ds(0, NS - 1)])
    sent(l_out, lsend.at[pl.ds(0, NS - 1)])

    assert recvs.n == N_RECV, recvs.n


def shards(
    patch_states, merge_in, merge_out, kv_weight, queries, new_kv, citations, lengths, prefill_owner, decode_owner
):
    along = (1, citations.shape[0])
    keys, asks = tables()
    vmem = pl.BlockSpec(memory_space=pltpu.VMEM)
    anywhere = pl.BlockSpec(memory_space=pl.ANY)
    result = pl.pallas_call(
        kernel,
        out_shape=jax.ShapeDtypeStruct((NS, 8 * HD), BF16),
        in_specs=[anywhere] * 4 + [vmem] * 6 + [anywhere, vmem],
        out_specs=vmem,
        scratch_shapes=[
            pltpu.VMEM((ROWS, KIN), BF16),
            pltpu.VMEM((2, GRID * GRID, HD), F32),
            pltpu.VMEM((TOKENS, KIN), BF16),
            pltpu.VMEM((KIN, HU), BF16),
            pltpu.VMEM((HU, 8192), BF16),
            pltpu.VMEM((8192, HD), BF16),
            pltpu.VMEM((HU, HD), F32),
            pltpu.VMEM((4, 2, HU, 2 * HD), BF16),
            pltpu.VMEM((2 * GROUP, HU), F32),
            pltpu.VMEM((4, GROUP, HU), BF16),
            pltpu.VMEM((4, 4, GROUP, 2 * HD), F32),
            pltpu.VMEM((4, 4, GROUP, 2 * HD), BF16),
            pltpu.VMEM((4, 4, GROUP, 2 * HD), BF16),
            pltpu.VMEM((12, GROUP, 2 * HD), BF16),
            pltpu.VMEM((12, GROUP, 2 * HD), BF16),
            pltpu.VMEM((TOKENS, HD), BF16),
            pltpu.VMEM((HD, TOKENS), BF16),
            pltpu.VMEM((4, 4, NS, 8 * HD), BF16),
            pltpu.VMEM((NS, HD, HD), BF16),
            pltpu.VMEM((NS + 1, 1, HD), F32),
            pltpu.VMEM((NS, HD, HD), BF16),
            pltpu.VMEM((NS, HD, HD), BF16),
            pltpu.VMEM((NS, 1, HD), F32),
            pltpu.VMEM((NS, 1, HD), F32),
            pltpu.SemaphoreType.DMA((N_SEND,)),
            pltpu.SemaphoreType.DMA((N_RECV,)),
            pltpu.SemaphoreType.DMA((N_LOCAL,)),
        ],
        compiler_params=pltpu.CompilerParams(
            collective_id=0, has_side_effects=True, vmem_limit_bytes=58 * 1024 * 1024
        ),
    )(
        patch_states, merge_in, merge_out, kv_weight, queries[0], new_kv[0],
        citations.T, lengths.reshape(along), prefill_owner.reshape(along), decode_owner.reshape(along),
        jnp.asarray(keys), jnp.asarray(asks),
    )
    return result[None]


def solution(mesh):
    return jax.shard_map(
        shards,
        mesh=mesh,
        in_specs=(
            P(("section", "tp"), None),
            P(None, "tp"),
            P("tp", None),
            P("tp", None),
            P("section", None, "tp"),
            P("section", None, "tp"),
            P(),
            P(),
            P(),
            P(),
        ),
        out_specs=P("section", None, "tp"),
        check_vma=False,
    )
```

```python
import math

import jax
import jax.numpy as jnp
import numpy as np
from jax import lax
from jax.experimental import pallas as pl
from jax.experimental.pallas import tpu as pltpu
from jax.sharding import PartitionSpec as P

F32 = jnp.float32
BF16 = jnp.bfloat16
VIT = 1280
HD = 128
GRID = 16
NS = 16
CITE = 4
ROWS = 64
GROUP = 128
TOKENS = 512
KIN = 5120
HU = 640
CHUNK = 1024
KVB = 1024
HALF = HU // 2
QUARTER = HU // 4


def tables():
    slot = np.arange(HD // 2)
    inverse = np.exp(slot.astype(np.float32) * np.float32(-2.0 * math.log(1000000.0) / HD)).astype(np.float32)
    token = np.arange(GRID * GRID)
    height = (token // GRID).astype(np.float32)
    across = (token % GRID).astype(np.float32)
    first = HD // 8
    second = first + 3 * HD // 16
    spatial = np.where(slot[None, :] < second, height[:, None], across[:, None])
    spatial = np.where(slot[None, :] < first, np.float32(0.0), spatial) * inverse[None, :]
    cosine, sine = np.cos(spatial), np.sin(spatial)
    keys = np.stack([np.concatenate([cosine, cosine], 1), np.concatenate([-sine, sine], 1)])
    steps = np.arange(CITE).astype(np.float32)[:, None] * inverse[None, :]
    steps = np.where(slot[None, :] < first, steps, np.float32(0.0))
    cosine, sine = np.cos(steps), np.sin(steps)
    asks = np.stack([np.concatenate([cosine, cosine], 1), np.concatenate([sine, -sine], 1)])
    return keys.astype(np.float32), asks.astype(np.float32)


class Counter:
    def __init__(self):
        self.n = 0

    def take(self, k=1):
        first = self.n
        self.n += k
        return first


N_SEND = 10
N_RECV = 110
N_LOCAL = 7


def kernel(
    patch_in, w1, w2, kvw, q, nkv, cites, lens, prefills, decodes, ktab_in, qtab, out,
    patch, ktab, rows, w1v, w2v, kvg, wacc, wg, hacc, hidb, mine, psend, precv, gsend, grecv,
    kbuf, vt, qg, askb, codeb, osend, orecv, lsend, lrecv, ssem, rsem, lsem,
):
    s = lax.axis_index("section")
    t = lax.axis_index("tp")
    x, c = t // 2, t % 2
    z, y = s // 4, s % 4
    mate = 2 * x + (1 - c)
    cr, cl, co = (x + 1) % 4, (x + 3) % 4, (x + 2) % 4
    xr, xl, xo = 2 * cr + c, 2 * cl + c, 2 * co + c
    yn, yp, yo = (y + 1) % 4, (y + 3) % 4, (y + 2) % 4
    zn, zp, zo = (z + 1) % 4, (z + 3) % 4, (z + 2) % 4
    recvs = Counter()
    kv_out, row_out, q_out, q_out_then, a_out, b_out, p_out, g_out, o_out, l_out = range(10)

    def to_tp(who):
        return {"tp": who}

    def to_section(who):
        return {"section": who}

    def remote(src, dst, kind, slot, dev):
        return pltpu.make_async_remote_copy(
            src_ref=src, dst_ref=dst, send_sem=ssem.at[kind], recv_sem=rsem.at[slot],
            device_id=dev, device_id_type=pl.DeviceIdType.MESH,
        )

    def start(src, dst, kind, slot, dev):
        remote(src, dst, kind, slot, dev).start()

    def arrive(dst, slot):
        remote(dst, dst, 0, slot, to_tp(mate)).wait_recv()

    def sent(kind, ref):
        remote(ref, ref, kind, 0, to_tp(mate)).wait_send()

    def sec(zz, yy):
        return to_section(zz * 4 + yy)

    barrier = pltpu.get_barrier_semaphore()
    neighbours = (to_tp(mate), to_tp(xr), to_tp(xl), sec(z, yn), sec(z, yp), sec(zn, y), sec(zp, y))
    for who in neighbours:
        pl.semaphore_signal(barrier, inc=1, device_id=who, device_id_type=pl.DeviceIdType.MESH)

    load1 = pltpu.make_async_copy(w1, w1v, lsem.at[0])
    load2 = pltpu.make_async_copy(w2, w2v, lsem.at[1])
    cols = pl.ds(pl.multiple_of(s * HD, HD), HD)

    def kv_at(b, h=None):
        if h is None:
            return kvg.at[pl.ds(pl.multiple_of(b * KVB, KVB), KVB), :]
        return kvg.at[pl.ds(pl.multiple_of(b * KVB + h * (KVB // 2), KVB // 2), KVB // 2), :]

    def rows_at(b, h=None):
        if h is None:
            return rows.at[pl.ds(pl.multiple_of(b * ROWS, ROWS), ROWS), :]
        return rows.at[pl.ds(pl.multiple_of(b * ROWS + h * (ROWS // 2), ROWS // 2), ROWS // 2), :]

    load3 = pltpu.make_async_copy(kvw.at[:, cols], kv_at(t), lsem.at[2])
    load4 = pltpu.make_async_copy(q, qg.at[z, y], lsem.at[3])
    load5 = pltpu.make_async_copy(patch_in, patch, lsem.at[5])
    load6 = pltpu.make_async_copy(ktab_in, ktab, lsem.at[6])
    load3.start()
    load4.start()
    load5.start()
    load2.start()
    load1.start()
    load6.start()

    load3.wait()
    pl.semaphore_wait(barrier, len(neighbours))

    class Ring:
        def __init__(self, at, kind):
            self.at, self.kind = at, kind
            self.base = recvs.take(10)

        def go(self, *rest):
            start(*rest[:2], self.kind, *rest[2:])

        def open(self, own):
            b = self.base
            self.go(own(0), self.at(t, 0), b + 0, to_tp(xr))
            self.go(own(1), self.at(t, 1), b + 3, to_tp(xl))
            self.go(own(1), self.at(t, 1), b + 1, to_tp(xr))
            self.go(own(0), self.at(t, 0), b + 2, to_tp(xl))
            self.go(own(None), self.at(t), b + 6, to_tp(mate))

        def forward(self):
            b = self.base
            arrive(self.at(xl, 0), b + 0)
            self.go(self.at(xl, 0), self.at(xl, 0), b + 4, to_tp(xr))
            arrive(self.at(xr, 1), b + 3)
            self.go(self.at(xr, 1), self.at(xr, 1), b + 5, to_tp(xl))

        def near(self):
            b = self.base
            arrive(self.at(xl, 1), b + 1)
            self.go(self.at(xl), self.at(xl), b + 7, to_tp(mate))
            arrive(self.at(xr, 0), b + 2)
            self.go(self.at(xr), self.at(xr), b + 8, to_tp(mate))

        def far(self):
            b = self.base
            arrive(self.at(xo, 0), b + 4)
            arrive(self.at(xo, 1), b + 5)
            self.go(self.at(xo), self.at(xo), b + 9, to_tp(mate))

        def mates(self, k):
            chip = (x, cl, cr, co)[k]
            arrive(self.at(2 * chip + (1 - c)), self.base + 6 + k)

    kv_ring = Ring(kv_at, kv_out)
    kv_ring.open(lambda h: kv_at(t, h))

    class Cross:
        def __init__(self, at, me, nxt, prv, opp, dev_n, dev_p, r0, half, kind):
            self.at, self.me, self.nxt, self.prv, self.opp = at, me, nxt, prv, opp
            self.dev_n, self.dev_p, self.r0, self.half, self.kind = dev_n, dev_p, r0, half, kind
            self.base = recvs.take(4)

        def low(self, k):
            return self.at(k, self.r0, self.half // 2)

        def high(self, k):
            return self.at(k, self.r0 + self.half // 2, self.half // 2)

        def open(self):
            own = self.at(self.me, self.r0, self.half)
            start(own, own, self.kind, self.base, self.dev_n)
            start(own, own, self.kind, self.base + 1, self.dev_p)

        def forward(self):
            b, low, high = self.base, self.low(self.prv), self.high(self.nxt)
            arrive(self.at(self.prv, self.r0, self.half), b)
            start(low, low, self.kind, b + 2, self.dev_n)
            arrive(self.at(self.nxt, self.r0, self.half), b + 1)
            start(high, high, self.kind, b + 3, self.dev_p)

        def finish(self):
            arrive(self.low(self.opp), self.base + 2)
            arrive(self.high(self.opp), self.base + 3)

    to_y = (y, yn, yp, yo, sec(z, yn), sec(z, yp))
    to_z = (z, zn, zp, zo, sec(zn, y), sec(zp, y))

    qy_first = Cross(lambda yy, r, n: qg.at[z, yy, :, pl.ds(r, n)], *to_y, 0, 512, q_out)
    qz_first = Cross(lambda zz, r, n: qg.at[zz, y, :, pl.ds(r, n)], *to_z, 512, 512, q_out)
    qz_then = Cross(lambda zz, r, n: qg.at[zz, :, :, pl.ds(r, n)], *to_z, 0, 512, q_out_then)
    qy_then = Cross(lambda yy, r, n: qg.at[:, yy, :, pl.ds(r, n)], *to_y, 512, 512, q_out_then)
    load4.wait()
    qy_first.open()
    qz_first.open()

    load5.wait()
    for b in range(KIN // VIT):
        span = pl.ds(b * VIT, VIT)
        block = patch[:, span].astype(F32)
        centered = block - jnp.mean(block, axis=-1, keepdims=True)
        variance = jnp.mean(centered * centered, axis=-1, keepdims=True)
        rows[pl.ds(pl.multiple_of(t * ROWS, ROWS), ROWS), span] = (
            centered * lax.rsqrt(variance + 1e-06)
        ).astype(BF16)

    lane = lax.broadcasted_iota(jnp.int32, (HD, HD), 1)
    sub = lax.broadcasted_iota(jnp.int32, (HD, HD), 0)
    eye = lane == sub

    def column(row):
        return jnp.sum(jnp.where(eye, row.astype(F32), 0.0), axis=1, keepdims=True)

    def heads_down(block):
        return jnp.concatenate([block[:, h * HD : (h + 1) * HD] for h in range(8)], axis=0)

    def windows():
        counts = lens[...]
        code = jnp.zeros((1, HD), jnp.int32)
        for j in range(CITE):
            cited = cites[j : j + 1, :]
            hit = (counts > j) & ((cited // 2) == s)
            code += jnp.where(hit, 1 + (cited % 2) + 2 * (counts - 1 - j), 0)
        code = column(code)
        owned = column(prefills[...]) == (lane % NS).astype(F32)
        decode = column(decodes[...])
        codeb[NS] = jnp.sum(
            jnp.where(owned & (decode == s.astype(F32)), 1.0, 0.0), axis=0, keepdims=True
        )

        @pl.loop(0, NS)
        def _(i):
            d = ((z + i // 4) % 4) * 4 + (y + i % 4) % 4
            row = jnp.sum(jnp.where(owned & (decode == d.astype(F32)), code, 0.0), axis=0, keepdims=True)
            codeb[i] = row

    def prepare():
        @pl.loop(0, NS)
        def _(i):
            col = column(codeb[i])
            cosine, sine = qtab[0, 0:1, :], qtab[1, 0:1, :]
            for p in range(1, CITE):
                now = (col == 1.0 + 2.0 * p) | (col == 2.0 + 2.0 * p)
                cosine = jnp.where(now, qtab[0, p : p + 1, :], cosine)
                sine = jnp.where(now, qtab[1, p : p + 1, :], sine)
            asks = heads_down(qg[(z + i // 4) % 4, (y + i % 4) % 4].astype(F32))
            askb[i] = (asks * cosine + pltpu.roll(asks, HD // 2, 1) * sine).astype(BF16)

    windows()

    def w_step(b, first=False):
        part = jnp.dot(
            w2v[:, pl.ds(pl.multiple_of(b * KVB, KVB), KVB)],
            kvg[pl.ds(pl.multiple_of(b * KVB, KVB), KVB), :],
            preferred_element_type=F32,
        )
        if first:
            wacc[...] = part
        else:
            wacc[...] += part

    load2.wait()
    w_step(t, first=True)
    kv_ring.mates(0)
    w_step(mate)
    kv_ring.forward()
    row_ring = Ring(rows_at, row_out)
    row_ring.open(lambda h: rows_at(t, h))
    qy_first.forward()
    qz_first.forward()
    kv_ring.near()
    w_step(xl)
    w_step(xr)
    kv_ring.mates(1)
    w_step(2 * cl + (1 - c))
    kv_ring.mates(2)
    w_step(2 * cr + (1 - c))
    qy_first.finish()
    qz_first.finish()
    qz_then.open()
    qy_then.open()
    kv_ring.far()
    w_step(xo)
    kv_ring.mates(3)
    w_step(2 * co + (1 - c))

    def lanes(yy):
        return pl.ds(pl.multiple_of((yy % 2) * HD, HD), HD)

    def block_at(zz, yy, r0, n):
        return wg.at[zz, yy // 2, pl.ds(r0, n), lanes(yy)]

    wg[z, y // 2, :, lanes(y)] = wacc[...].astype(BF16)

    class Spread:
        def __init__(self, at, first, second, kind):
            self.at, self.kind = at, kind
            self.p, self.pn, self.pp, self.po, self.dev1n, self.dev1p = first
            self.q, self.qn, self.qp, self.qo, self.dev2n, self.dev2p = second
            self.along = (self.p, self.pp, self.pn, self.po)
            self.base = recvs.take(20)

        def whole(self, p, q):
            return self.at(p, q, 0, HALF)

        def low(self, p, q):
            return self.at(p, q, 0, QUARTER)

        def high(self, p, q):
            return self.at(p, q, QUARTER, QUARTER)

        def go(self, ref, slot, dev):
            start(ref, ref, self.kind, self.base + slot, dev)

        def across(self, k):
            block = self.whole(self.along[k], self.q)
            self.go(block, 4 + 4 * k, self.dev2n)
            self.go(block, 5 + 4 * k, self.dev2p)

        def open(self):
            block = self.whole(self.p, self.q)
            self.go(block, 0, self.dev1n)
            self.go(block, 1, self.dev1p)

        def near(self):
            arrive(self.whole(self.pp, self.q), self.base)
            self.go(self.low(self.pp, self.q), 2, self.dev1n)
            arrive(self.whole(self.pn, self.q), self.base + 1)
            self.go(self.high(self.pn, self.q), 3, self.dev1p)

        def far(self):
            arrive(self.low(self.po, self.q), self.base + 2)
            arrive(self.high(self.po, self.q), self.base + 3)
            self.across(3)

        def turn(self, k):
            p = self.along[k]
            arrive(self.whole(p, self.qp), self.base + 4 + 4 * k)
            self.go(self.low(p, self.qp), 6 + 4 * k, self.dev2n)
            arrive(self.whole(p, self.qn), self.base + 5 + 4 * k)
            self.go(self.high(p, self.qn), 7 + 4 * k, self.dev2p)

        def finish(self):
            for k in range(4):
                p = self.along[k]
                arrive(self.low(p, self.qo), self.base + 6 + 4 * k)
                arrive(self.high(p, self.qo), self.base + 7 + 4 * k)

    upper = Spread(lambda yy, zz, r, n: block_at(zz, yy, r, n), to_y, to_z, a_out)
    lower = Spread(lambda zz, yy, r, n: block_at(zz, yy, HALF + r, n), to_z, to_y, b_out)
    upper.open()
    lower.open()
    upper.across(0)
    lower.across(0)

    far_base = recvs.take(KIN // CHUNK)

    def far_part(b, k):
        return rows_at(b).at[:, pl.ds(k * CHUNK, CHUNK)]

    def far_rows():
        arrive(rows_at(xo, 0), row_ring.base + 4)
        arrive(rows_at(xo, 1), row_ring.base + 5)
        for k in range(KIN // CHUNK):
            start(far_part(xo, k), far_part(xo, k), row_out, far_base + k, to_tp(mate))

    def far_ready(k):
        arrive(far_part(2 * co + (1 - c), k), far_base + k)

    def hidden(*groups, ready=None):
        spans = [pl.ds(pl.multiple_of(g * GROUP, GROUP), GROUP) for g in groups]
        used = pl.ds(0, len(groups) * GROUP)

        def part(k):
            span = pl.ds(pl.multiple_of(k * CHUNK, CHUNK), CHUNK)
            left = jnp.concatenate([rows[r, span] for r in spans], axis=0)
            return jnp.dot(left, w1v[span, :], preferred_element_type=F32)

        if ready is None:
            hacc[used] = part(0)

            @pl.loop(1, KIN // CHUNK)
            def _(k):
                hacc[used] += part(k)
        else:
            for k in range(KIN // CHUNK):
                ready(k)
                if k == 0:
                    hacc[used] = part(k)
                else:
                    hacc[used] += part(k)

        for n, g in enumerate(groups):
            pre = hacc[n * GROUP : (n + 1) * GROUP]
            hidb[g] = (0.5 * pre * (1.0 + lax.erf(pre * np.float32(math.sqrt(0.5))))).astype(BF16)

    p_base = recvs.take(16)
    g_base = recvs.take(11)
    order = (x, cl, cr, co)
    dests = (co, cr, cl, x)

    def pair_copy(k, n):
        g = order[k]
        return remote(psend.at[g, n], precv.at[g, n], p_out, p_base + 4 * k + n, to_tp(mate))

    lower_rows, upper_rows = pl.ds(0, ROWS), pl.ds(ROWS, ROWS)
    A_R, A_L, B_R, B_L, C_L, C_R, E_R, E_L, F_R, F_L, F_O = range(11)
    places = {
        A_R: (0, lower_rows), A_L: (0, upper_rows), B_R: (1,), B_L: (2,), C_L: (pl.ds(3, 2),), C_R: (pl.ds(5, 2),),
        E_R: (7,), E_L: (8,), F_R: (9,), F_L: (10,), F_O: (11,),
    }

    def relay(m):
        who = {A_R: xr, B_R: xr, C_R: xr, E_R: xr, F_R: xr, F_O: xo}.get(m, xl)
        return remote(gsend.at[places[m]], grecv.at[places[m]], g_out, g_base + m, to_tp(who))

    def project(k):
        hid = hidb[order[k]]
        for n in range(4):
            psend[order[k], n] = jnp.dot(hid, wg[dests[n], 1 - c], preferred_element_type=F32).astype(BF16)
            pair_copy(k, n).start()
        for n in range(4):
            mine[order[k], n] = jnp.dot(hid, wg[dests[n], c], preferred_element_type=F32)

    def pair_sum(k):
        g = order[k]
        out_now = (
            {0: None},
            {0: 3, 2: 4},
            {0: 5, 1: 6},
            {0: 11, 1: 9, 2: 10},
        )[k]
        after = ({0: (A_R, A_L)}, {2: (C_L,)}, {1: (C_R,)}, {0: (F_O,), 1: (F_R,), 2: (F_L,)})[k]
        for n in range(4):
            pair_copy(k, n).wait_recv()
            total = mine[g, n] + precv[g, n].astype(F32)
            if n not in out_now:
                mine[g, n] = total
            else:
                gsend[out_now[n] or 0] = total.astype(BF16)
            for m in after.get(n, ()):
                relay(m).start()

    def pass_halves():
        relay(A_R).wait_recv()
        gsend[7, :ROWS] = (mine[cl, 1, :ROWS] + grecv[0, :ROWS].astype(F32)).astype(BF16)
        gsend[7, ROWS:] = mine[cl, 1, ROWS:].astype(BF16)
        relay(E_R).start()
        relay(A_L).wait_recv()
        gsend[8, :ROWS] = mine[cr, 2, :ROWS].astype(BF16)
        gsend[8, ROWS:] = (mine[cr, 2, ROWS:] + grecv[0, ROWS:].astype(F32)).astype(BF16)
        relay(E_L).start()

    def pass_on():
        relay(C_R).wait_recv()
        gsend[1] = (mine[x, 1] + grecv[5].astype(F32)).astype(BF16)
        relay(B_R).start()
        relay(C_L).wait_recv()
        gsend[2] = (mine[x, 2] + grecv[3].astype(F32)).astype(BF16)
        relay(B_L).start()

    def last(k):
        g = order[k]
        total = mine[g, 3]
        for m, n in (((F_O, 11), (None, 4), (None, 6)), ((B_R, 1), (F_L, 10)), ((B_L, 2), (F_R, 9)), ((E_R, 7), (E_L, 8)))[k]:
            if m is not None:
                relay(m).wait_recv()
            total += grecv[n].astype(F32)
        key = total[:, :HD]
        r = pl.ds(pl.multiple_of(g * GROUP, GROUP), GROUP)
        place = pl.ds(pl.multiple_of((g % 2) * GROUP, GROUP), GROUP)
        kbuf[r, :] = (key * ktab[0, place, :] + pltpu.roll(key, HD // 2, 1) * ktab[1, place, :]).astype(BF16)
        vt[:, r] = total[:, HD:].T.astype(BF16)

    load1.wait()
    row_ring.mates(0)
    hidden(x)
    upper.near()
    lower.near()
    for k in (1, 2):
        upper.across(k)
        lower.across(k)
    upper.turn(0)
    lower.turn(0)
    upper.far()
    lower.far()
    row_ring.forward()
    upper.turn(1)
    lower.turn(1)
    upper.turn(2)
    lower.turn(2)
    qz_then.forward()
    qy_then.forward()
    row_ring.near()
    upper.turn(3)
    lower.turn(3)
    row_ring.mates(1)
    row_ring.mates(2)
    hidden(cl, cr)
    qz_then.finish()
    qy_then.finish()
    upper.finish()
    lower.finish()
    project(0)
    project(1)
    pair_sum(0)
    project(2)
    pair_sum(1)
    pair_sum(2)
    far_rows()
    pass_halves()
    hidden(co, ready=far_ready)
    project(3)
    pass_on()
    pair_sum(3)
    prepare()
    load6.wait()
    for k in (1, 2, 3, 0):
        last(k)

    inv_root = np.float32(1.0 / math.sqrt(HD))
    o_base = recvs.take(2)

    def place(i):
        return ((z + i // 4) % 4) * 4 + (y + i % 4) % 4

    def scores_of(sections):
        asks = jnp.concatenate([askb[i] for i in sections], axis=0)
        return lax.dot_general(kbuf[...], asks, (((1,), (1,)), ((), ())), preferred_element_type=F32)

    def part_of(sections, scores):
        row = jnp.concatenate([codeb[i] for i in sections], axis=1)
        second = (row == 2.0) | (row == 4.0) | (row == 6.0) | (row == 8.0)
        frame = jnp.where(second, scores[256:], scores[:256]) * inv_root
        top = jnp.max(frame, axis=0, keepdims=True)
        weight = jnp.exp(frame - top)
        total = jnp.sum(weight, axis=0, keepdims=True)
        both = jnp.concatenate([jnp.where(second, 0.0, weight), jnp.where(second, weight, 0.0)], axis=0)
        value = jnp.dot(vt[...], both.astype(BF16), preferred_element_type=F32) / total
        live = row > 0.0
        value = jnp.where(live, value, 0.0).astype(BF16)
        level = jnp.where(live, top + jnp.log(total), -1e30)
        for k, i in enumerate(sections):
            osend[place(i)] = value[:, k * HD : (k + 1) * HD]
            lsend[place(i)] = level[:, k * HD : (k + 1) * HD]

    def part_copies(i):
        d = place(i)
        who = to_section(d)
        return (
            remote(lsend.at[d], lrecv.at[s], l_out, o_base + 1, who),
            remote(osend.at[d], orecv.at[s], o_out, o_base, who),
        )

    turns = ((10, 9, 11, 6), (14, 5, 15, 7), (13, 8, 2, 4), (12, 1, 3, 0))
    scores = scores_of(turns[0])
    for n, sections in enumerate(turns):
        now = scores
        if n + 1 < len(turns):
            scores = scores_of(turns[n + 1])
        part_of(sections, now)
        for i in sections:
            if i > 0:
                for copy in part_copies(i):
                    copy.start()
    orecv[s] = osend[s]
    lrecv[s] = lsend[s]

    asks = heads_down(q[...].astype(F32)).astype(BF16)
    own = lax.dot_general(nkv[:, :HD], asks, (((1,), (1,)), ((), ())), preferred_element_type=F32)
    pick = (lax.broadcasted_iota(jnp.int32, (NS, HD), 1) % NS) == lax.broadcasted_iota(jnp.int32, (NS, HD), 0)
    own = jnp.sum(jnp.where(pick, own, 0.0), axis=0, keepdims=True) * inv_root
    value = nkv[:, HD:].astype(F32)
    value = jnp.concatenate([value] * 8, axis=0).T
    present = codeb[NS]

    arrive(lrecv.at[pl.ds(0, NS - 1)], o_base + 1)
    arrive(orecv.at[pl.ds(0, NS - 1)], o_base)

    level = [lrecv[j] for j in range(NS)]
    top = own
    for v in level:
        top = jnp.maximum(top, v)
    weight = jnp.exp(own - top)
    total, value = weight, value * weight
    for j in range(NS):
        weight = jnp.exp(level[j] - top)
        total += weight
        value += orecv[j].astype(F32) * weight
    value = jnp.where(present > 0.0, value / total, 0.0).T
    for h in range(8):
        out[:, h * HD : (h + 1) * HD] = value[h * NS : (h + 1) * NS, :].astype(BF16)

    units = 15 * HALF
    sent(kv_out, kvg.at[pl.ds(0, 7 * KVB), :])
    sent(row_out, rows.at[pl.ds(0, 7 * ROWS), :])
    sent(q_out, qg.at[0, pl.ds(0, 3)])
    sent(q_out_then, qg.at[pl.ds(0, 3)])
    sent(a_out, kvg.at[pl.ds(0, units), :])
    sent(b_out, kvg.at[pl.ds(0, units), :])
    sent(p_out, psend)
    sent(g_out, gsend)
    sent(o_out, osend.at[pl.ds(0, NS - 1)])
    sent(l_out, lsend.at[pl.ds(0, NS - 1)])

    assert recvs.n == N_RECV, recvs.n


def shards(
    patch_states, merge_in, merge_out, kv_weight, queries, new_kv, citations, lengths, prefill_owner, decode_owner
):
    along = (1, citations.shape[0])
    keys, asks = tables()
    vmem = pl.BlockSpec(memory_space=pltpu.VMEM)
    anywhere = pl.BlockSpec(memory_space=pl.ANY)
    result = pl.pallas_call(
        kernel,
        out_shape=jax.ShapeDtypeStruct((NS, 8 * HD), BF16),
        in_specs=[anywhere] * 4 + [vmem] * 6 + [anywhere, vmem],
        out_specs=vmem,
        scratch_shapes=[
            pltpu.VMEM((ROWS, KIN), BF16),
            pltpu.VMEM((2, GRID * GRID, HD), F32),
            pltpu.VMEM((TOKENS, KIN), BF16),
            pltpu.VMEM((KIN, HU), BF16),
            pltpu.VMEM((HU, 8192), BF16),
            pltpu.VMEM((8192, HD), BF16),
            pltpu.VMEM((HU, HD), F32),
            pltpu.VMEM((4, 2, HU, 2 * HD), BF16),
            pltpu.VMEM((2 * GROUP, HU), F32),
            pltpu.VMEM((4, GROUP, HU), BF16),
            pltpu.VMEM((4, 4, GROUP, 2 * HD), F32),
            pltpu.VMEM((4, 4, GROUP, 2 * HD), BF16),
            pltpu.VMEM((4, 4, GROUP, 2 * HD), BF16),
            pltpu.VMEM((12, GROUP, 2 * HD), BF16),
            pltpu.VMEM((12, GROUP, 2 * HD), BF16),
            pltpu.VMEM((TOKENS, HD), BF16),
            pltpu.VMEM((HD, TOKENS), BF16),
            pltpu.VMEM((4, 4, NS, 8 * HD), BF16),
            pltpu.VMEM((NS, HD, HD), BF16),
            pltpu.VMEM((NS + 1, 1, HD), F32),
            pltpu.VMEM((NS, HD, HD), BF16),
            pltpu.VMEM((NS, HD, HD), BF16),
            pltpu.VMEM((NS, 1, HD), F32),
            pltpu.VMEM((NS, 1, HD), F32),
            pltpu.SemaphoreType.DMA((N_SEND,)),
            pltpu.SemaphoreType.DMA((N_RECV,)),
            pltpu.SemaphoreType.DMA((N_LOCAL,)),
        ],
        compiler_params=pltpu.CompilerParams(
            collective_id=0, has_side_effects=True, vmem_limit_bytes=58 * 1024 * 1024
        ),
    )(
        patch_states, merge_in, merge_out, kv_weight, queries[0], new_kv[0],
        citations.T, lengths.reshape(along), prefill_owner.reshape(along), decode_owner.reshape(along),
        jnp.asarray(keys), jnp.asarray(asks),
    )
    return result[None]


def solution(mesh):
    return jax.shard_map(
        shards,
        mesh=mesh,
        in_specs=(
            P(("section", "tp"), None),
            P(None, "tp"),
            P("tp", None),
            P("tp", None),
            P("section", None, "tp"),
            P("section", None, "tp"),
            P(),
            P(),
            P(),
            P(),
        ),
        out_specs=P("section", None, "tp"),
        check_vma=False,
    )
```
